32 devices in a mesh: row: 8 (over z, x), col: 4 (over y, core).
Axes of the slice: x: 2, y: 2, z: 4, core: 2. Of those that a mesh axis runs over, the one named last changes fastest.
Arguments:
- inputs: bfloat16 [768, 8192], P(None, 'row'), may hold values from -6 to 6
- out_grad: bfloat16 [768, 8192], P(None, 'col'), may hold values from -6 to 6
- gate_weight: bfloat16 [8192, 14336], P('row', 'col'), may hold values from -0.09375 to 0.09375
- up_weight: bfloat16 [8192, 14336], P('row', 'col'), may hold values from -0.09375 to 0.09375
- down_weight: bfloat16 [14336, 8192], P('row', 'col'), may hold values from -0.0625 to 0.0625
- gate_mask: int32 [64, 112], P('row', 'col'), may hold values 0 or 1
- up_mask: int32 [64, 112], P('row', 'col'), may hold values 0 or 1
- down_mask: int32 [112, 64], P('row', 'col'), may hold values 0 or 1
Outputs:
- input_grad: bfloat16 [768, 8192], P(None, 'row')
- gate_grad: bfloat16 [8192, 14336], P('row', 'col')
- up_grad: bfloat16 [8192, 14336], P('row', 'col')
- down_grad: bfloat16 [14336, 8192], P('row', 'col')
The draws below stay inside these ranges and needn't reach their ends.
All inputs are finite; a program needn't handle non-finite values. No bound on the sum of `gate_mask` or of `up_mask` or of `down_mask` on one device may be relied on, other than what follows from the above.
Results may differ from the reference program's by a relative error of at most 0.0068.
Values may be sent and summed in bfloat16 or wider, within the bound.
No kernel may reach another device: no remote copies, remote signals or barrier semaphores. Data moves between devices by JAX's collectives and lax.ppermute only.
A program may use at most 256 MiB of HBM per device.

```python
import jax
import jax.numpy as jnp

D = 8192
FF = 14336
BLOCK = 128
TOK = 768


def set_ends(entries, key, smallest, top_value):
    shape = entries.shape
    spot = [jax.random.randint(jax.random.fold_in(key, axis), (), 0, shape[axis]) for axis in range(len(shape))]
    entries = entries.at[tuple(spot)].set(smallest)
    longest = shape.index(max(shape))
    spot[longest] = (spot[longest] + 1) % shape[longest]
    return entries.at[tuple(spot)].set(top_value)


def levels(stream_key, extent, split, least, top_value):
    factor_of = 1.0
    for axis_at, shards_of in split:
        steps = jax.random.uniform(jax.random.fold_in(jax.random.fold_in(stream_key, 6), axis_at), (shards_of,), jnp.float32, least / len(split), top_value / len(split))
        factor_of = factor_of * jnp.repeat(jnp.exp(steps), extent[axis_at] // shards_of).reshape((-1,) + (1,) * (len(extent) - 1 - axis_at))
    return factor_of


def normal_values(key, shape, spread, reach, cuts=(), kind=jnp.bfloat16):
    result = jax.random.normal(key, shape, jnp.float32) * spread
    if len(cuts) > 0:
        result = levels(key, shape, cuts, -0.22, 0.18) * result
    return jnp.clip(result, min=-reach, max=reach).astype(kind)


def setup_inputs(seed: int = 0) -> dict:
    splits = jax.random.split(jax.random.key(seed), 9)
    inputs = normal_values(splits[0], (TOK, D), 1.0, 6.0, ((1, 8),))
    out_grad = normal_values(splits[1], (TOK, D), 1.0, 6.0, ((1, 4),))
    gate_weight = normal_values(splits[2], (D, FF), (D // 2) ** -0.5, 0.09375, ((0, 8), (1, 4)))
    up_weight = normal_values(splits[3], (D, FF), (D // 2) ** -0.5, 0.09375, ((0, 8), (1, 4)))
    down_weight = normal_values(splits[4], (FF, D), (FF // 2) ** -0.5, 0.0625, ((0, 8), (1, 4)))
    gate_mask = set_ends((jax.random.randint(splits[5], (D // BLOCK, FF // BLOCK), 0, 2) < 1).astype(jnp.int32), jax.random.fold_in(splits[5], 1), 0, 1)
    up_mask = set_ends((jax.random.randint(splits[6], (D // BLOCK, FF // BLOCK), 0, 2) < 1).astype(jnp.int32), jax.random.fold_in(splits[6], 1), 0, 1)
    down_mask = set_ends((jax.random.randint(splits[7], (FF // BLOCK, D // BLOCK), 0, 2) < 1).astype(jnp.int32), jax.random.fold_in(splits[7], 1), 0, 1)
    return dict(inputs=inputs, out_grad=out_grad, gate_weight=gate_weight, up_weight=up_weight, down_weight=down_weight, gate_mask=gate_mask, up_mask=up_mask, down_mask=down_mask)


def expand(mask):
    return jnp.repeat(jnp.repeat(mask, BLOCK, axis=0), BLOCK, axis=1).astype(jnp.bfloat16)


def reference(inputs, out_grad, gate_weight, up_weight, down_weight, gate_mask, up_mask, down_mask):
    gate_eff = gate_weight * expand(gate_mask)
    up_eff = up_weight * expand(up_mask)
    down_eff = down_weight * expand(down_mask)
    gate = jnp.dot(inputs, gate_eff, preferred_element_type=jnp.float32).astype(jnp.bfloat16)
    up = jnp.dot(inputs, up_eff, preferred_element_type=jnp.float32).astype(jnp.bfloat16)
    gate_f = gate.astype(jnp.float32)
    up_f = up.astype(jnp.float32)
    sig = jax.nn.sigmoid(gate_f)
    hidden = (gate_f * sig * up_f).astype(jnp.bfloat16)
    hidden_grad = jnp.dot(out_grad, down_eff.T, preferred_element_type=jnp.float32)
    gate_delta = (hidden_grad * up_f * sig * (1.0 + gate_f * (1.0 - sig))).astype(jnp.bfloat16)
    up_delta = (hidden_grad * gate_f * sig).astype(jnp.bfloat16)
    down_grad = (jnp.dot(hidden.T, out_grad, preferred_element_type=jnp.float32) * expand(down_mask).astype(jnp.float32)).astype(jnp.bfloat16)
    gate_grad = (jnp.dot(inputs.T, gate_delta, preferred_element_type=jnp.float32) * expand(gate_mask).astype(jnp.float32)).astype(jnp.bfloat16)
    up_grad = (jnp.dot(inputs.T, up_delta, preferred_element_type=jnp.float32) * expand(up_mask).astype(jnp.float32)).astype(jnp.bfloat16)
    input_grad = (jnp.dot(gate_delta, gate_eff.T, preferred_element_type=jnp.float32) + jnp.dot(up_delta, up_eff.T, preferred_element_type=jnp.float32)).astype(jnp.bfloat16)
    return input_grad, gate_grad, up_grad, down_grad
```

```python
import functools

import jax
import jax.numpy as jnp
from jax import lax
from jax.experimental import pallas as pl
from jax.experimental.pallas import tpu as pltpu
from jax.sharding import PartitionSpec as P

BLOCK = 128
ROWS = 16
BF16 = jnp.bfloat16
F32 = jnp.float32


def params(**more):
    return pltpu.CompilerParams(vmem_limit_bytes=50 * 1024 * 1024, **more)


def cost(flops, bytes_accessed):
    return pl.CostEstimate(flops=int(flops), bytes_accessed=int(bytes_accessed), transcendentals=0)


def widen(mask):
    return jnp.repeat(jnp.repeat(mask.astype(BF16), BLOCK, axis=1), ROWS, axis=0)


def masked(value, wide):
    rows, columns = value.shape
    blocks = rows // BLOCK
    spread = jnp.broadcast_to(
        wide.reshape(blocks, 1, ROWS, columns), (blocks, BLOCK // ROWS, ROWS, columns)
    )
    return value * spread.reshape(rows, columns)


def dot_nt(left, right):
    return lax.dot_general(left, right, (((1,), (1,)), ((), ())), preferred_element_type=F32)


def tile_of(size, most):
    best = BLOCK
    for tile in range(BLOCK, most + 1, BLOCK):
        if size % tile == 0:
            best = tile
    return best


def piece_kernel(at, x_ref, w_ref, m_ref, *rest):
    *came, out_ref, total_ref = rest
    term = jnp.dot(x_ref[...], masked(w_ref[...], m_ref[...]), preferred_element_type=F32)

    @pl.when(pl.program_id(0) == 0)
    def _():
        start = term
        for ref in came:
            start = start + ref[...].astype(F32)
        total_ref[...] = start

    @pl.when(pl.program_id(0) > 0)
    def _():
        total_ref[...] += term

    @pl.when(pl.program_id(0) == pl.num_programs(0) - 1)
    def _():
        out_ref[...] = total_ref[...].astype(out_ref.dtype)


def piece(at, inputs, weight, wide, came, tokens, columns, kind):
    depth = inputs.shape[1]
    tile = tile_of(depth, 256)
    whole = pl.BlockSpec((tokens, columns), lambda k, at: (0, 0))
    return pl.pallas_call(
        piece_kernel,
        out_shape=jax.ShapeDtypeStruct((tokens, columns), kind),
        grid_spec=pltpu.PrefetchScalarGridSpec(
            num_scalar_prefetch=1,
            grid=(depth // tile,),
            in_specs=[
                pl.BlockSpec((tokens, tile), lambda k, at: (at[0], k)),
                pl.BlockSpec((tile, columns), lambda k, at: (k, at[1])),
                pl.BlockSpec((tile // BLOCK * ROWS, columns), lambda k, at: (k, at[1])),
            ]
            + [whole] * len(came),
            out_specs=whole,
            scratch_shapes=[pltpu.VMEM((tokens, columns), F32)],
        ),
        compiler_params=params(),
        cost_estimate=cost(2 * tokens * depth * columns, 2 * depth * columns + 6 * tokens * columns),
    )(at, inputs, weight, wide, *came)


def hidden_grad_kernel(g_ref, w_ref, m_ref, out_ref):
    weight = masked(w_ref[...], m_ref[...])
    parts, tokens, _ = out_ref.shape
    first = pl.program_id(1) == 0
    for t in range(parts):
        term = dot_nt(g_ref[t * tokens : (t + 1) * tokens, :], weight)

        @pl.when(first)
        def _():
            out_ref[t] = term

        @pl.when(jnp.logical_not(first))
        def _():
            out_ref[t] += term


def hidden_grad_partial(out_grad, weight, wide, parts, columns):
    count, depth = out_grad.shape
    cuts = weight.shape[0] // columns
    tokens = count // parts
    tile = tile_of(depth, 512)
    return pl.pallas_call(
        hidden_grad_kernel,
        out_shape=jax.ShapeDtypeStruct((cuts * parts, tokens, columns), F32),
        grid=(cuts, depth // tile),
        in_specs=[
            pl.BlockSpec((count, tile), lambda i, k: (0, k)),
            pl.BlockSpec((columns, tile), lambda i, k: (i, k)),
            pl.BlockSpec((columns // BLOCK * ROWS, tile), lambda i, k: (i, k)),
        ],
        out_specs=pl.BlockSpec((parts, tokens, columns), lambda i, k: (i, 0, 0)),
        compiler_params=params(),
        cost_estimate=cost(2 * count * depth * weight.shape[0], 2 * weight.size + 2 * out_grad.size + 4 * count * weight.shape[0]),
    )(out_grad, weight, wide)


def input_grad_kernel(at, sum_ref, gd_ref, ud_ref, gw_ref, uw_ref, gm_ref, um_ref, out_ref):
    term = dot_nt(gd_ref[...], masked(gw_ref[...], gm_ref[...]))
    term = term + dot_nt(ud_ref[...], masked(uw_ref[...], um_ref[...]))
    out_ref[0] = sum_ref[0] + term


def add_input_grad(at, total, gate_delta, up_delta, gate_weight, up_weight, gate_wide, up_wide):
    tokens, columns = gate_delta.shape
    depth = gate_weight.shape[0]
    tile = tile_of(depth, 256)
    delta = pl.BlockSpec((tokens, columns), lambda n, at: (0, 0))
    weight = pl.BlockSpec((tile, columns), lambda n, at: (n, at[1]))
    wide = pl.BlockSpec((tile // BLOCK * ROWS, columns), lambda n, at: (n, at[1]))
    sums = pl.BlockSpec((1, tokens, tile), lambda n, at: (at[0], 0, n))
    return pl.pallas_call(
        input_grad_kernel,
        out_shape=jax.ShapeDtypeStruct(total.shape, F32),
        grid_spec=pltpu.PrefetchScalarGridSpec(
            num_scalar_prefetch=1,
            grid=(depth // tile,),
            in_specs=[sums, delta, delta, weight, weight, wide, wide],
            out_specs=sums,
        ),
        input_output_aliases={1: 0},
        compiler_params=params(),
        cost_estimate=cost(4 * tokens * depth * columns, 4 * depth * columns + 8 * tokens * depth),
    )(at, total, gate_delta, up_delta, gate_weight, up_weight, gate_wide, up_wide)


def weight_grads_kernel(parts, at, *refs):
    lefts, gates, ups = refs[:parts], refs[parts : 2 * parts], refs[2 * parts : 3 * parts]
    gm_ref, um_ref, gate_ref, up_ref = refs[3 * parts], refs[3 * parts + 1], refs[-2], refs[-1]
    for deltas, m_ref, out_ref in ((gates, gm_ref, gate_ref), (ups, um_ref, up_ref)):
        total = None
        for left, delta in zip(lefts, deltas):
            term = jnp.dot(left[0], delta[...], preferred_element_type=F32)
            total = term if total is None else total + term
        out_ref[...] = masked(total.astype(BF16), m_ref[...])


def weight_grads(at, inputs_t, gates, ups, gate_wide, up_wide, width, before):
    _, depth, tokens = inputs_t.shape
    parts, columns = len(gates), gates[0].shape[1]
    tile = tile_of(depth, 256)
    lefts = [
        pl.BlockSpec((1, tile, tokens), lambda m, at, i=i: (at[1 + i], m, 0)) for i in range(parts)
    ]
    delta = pl.BlockSpec((tokens, columns), lambda m, at: (0, 0))
    wide = pl.BlockSpec((tile // BLOCK * ROWS, columns), lambda m, at: (m, at[0]))
    out = pl.BlockSpec((tile, columns), lambda m, at: (m, at[0]))
    shape = jax.ShapeDtypeStruct((depth, width), BF16)
    operands = [inputs_t] * parts + gates + ups + [gate_wide, up_wide]
    specs = lefts + [delta] * (2 * parts) + [wide, wide]
    aliases = {}
    if before is not None:
        aliases = {1 + len(operands): 0, 2 + len(operands): 1}
        operands = operands + list(before)
        specs = specs + [pl.BlockSpec(memory_space=pl.ANY)] * 2
    return pl.pallas_call(
        functools.partial(weight_grads_kernel, parts),
        out_shape=(shape, shape),
        grid_spec=pltpu.PrefetchScalarGridSpec(
            num_scalar_prefetch=1,
            grid=(depth // tile,),
            in_specs=specs,
            out_specs=(out, out),
        ),
        input_output_aliases=aliases,
        compiler_params=params(),
        cost_estimate=cost(4 * parts * tokens * depth * columns, 4 * depth * columns + 4 * parts * tokens * columns),
    )(at, *operands)


def down_grad_kernel(h_ref, g_ref, m_ref, out_ref):
    parts, _, tokens = h_ref.shape
    total = None
    for t in range(parts):
        term = jnp.dot(h_ref[t], g_ref[t * tokens : (t + 1) * tokens, :], preferred_element_type=F32)
        total = term if total is None else total + term
    out_ref[...] = masked(total.astype(BF16), m_ref[...])


def down_grad_of(hidden_t, out_grad, wide, parts):
    pieces, columns, tokens = hidden_t.shape
    cuts = pieces // parts
    count, width = out_grad.shape
    tile = tile_of(width, 512)
    return pl.pallas_call(
        down_grad_kernel,
        out_shape=jax.ShapeDtypeStruct((cuts * columns, width), BF16),
        grid=(cuts, width // tile),
        in_specs=[
            pl.BlockSpec((parts, columns, tokens), lambda i, j: (i, 0, 0)),
            pl.BlockSpec((count, tile), lambda i, j: (0, j)),
            pl.BlockSpec((columns // BLOCK * ROWS, tile), lambda i, j: (i, j)),
        ],
        out_specs=pl.BlockSpec((columns, tile), lambda i, j: (i, j)),
        compiler_params=params(),
        cost_estimate=cost(2 * count * cuts * columns * width, 2 * cuts * columns * width + 2 * out_grad.size),
    )(hidden_t, out_grad, wide)


def on_device(rows, cols, inputs, out_grad, gate_weight, up_weight, down_weight, gate_mask, up_mask, down_mask):
    count, depth = inputs.shape
    width = gate_weight.shape[1]
    ratio = rows // cols

    lines = rows // 4 if rows % 4 == 0 else 1
    length = rows // lines
    ring = []
    for line in range(lines):
        steps = range(length) if line % 2 == 0 else range(length - 1, -1, -1)
        ring += [step * lines + line for step in steps]
    place = [ring.index(r) for r in range(rows)]
    ahead = [(ring[p], ring[(p + 1) % rows]) for p in range(rows)]
    back = [(b, a) for a, b in ahead]
    me = jnp.array(place, jnp.int32)[lax.axis_index("row")]

    cuts = max(
        q for q in range(ratio, rows // 2 + 1, ratio) if rows % q == 0 and width // BLOCK % q == 0
    )
    parts = rows // cuts
    tokens, columns = count // parts, width // cuts
    far, near = rows // 2, rows - 1 - rows // 2

    def where_is(shard):
        shard = lax.rem(shard + 2 * rows, rows)
        return jnp.stack([shard // cuts, lax.rem(shard, cuts)])

    meet = []
    for r in range(rows):
        for c in range(cols):
            shard = (c % parts) * cuts + r % ratio * (cuts // ratio) + c // parts
            meet.append((r * cols + c, ring[shard] * cols + r // ratio))
    meet_back = [(b, a) for a, b in meet]

    gate_wide, up_wide, down_wide = widen(gate_mask), widen(up_mask), widen(down_mask)
    gate_set, up_set = (gate_weight, gate_wide), (up_weight, up_wide)

    def part(which, shard, came, kind=BF16):
        return piece(where_is(shard), inputs, *which, came, tokens, columns, kind)

    def onward(value):
        return lax.ppermute(value, "row", ahead)

    def backward(value):
        return lax.ppermute(value, "row", back)

    gate_on, up_back = part(gate_set, me + far, []), part(up_set, me - far, [])
    up_on, gate_back = part(up_set, me + near, []), part(gate_set, me - near, [])
    out_grad, gate_on, up_back, up_on, gate_back = lax.optimization_barrier(
        (out_grad, gate_on, up_back, up_on, gate_back)
    )
    hidden_grad = hidden_grad_partial(out_grad, down_weight, down_wide, parts, columns)
    hidden_grad = lax.psum_scatter(hidden_grad, "col", scatter_dimension=0, tiled=False)
    hidden_grad = lax.ppermute(hidden_grad.astype(BF16), ("row", "col"), meet)
    for step in range(1, far + 1):
        gate_on, up_back = onward(gate_on), backward(up_back)
        if step <= near:
            up_on, gate_back = onward(up_on), backward(gate_back)
        if step < far:
            gate_on = part(gate_set, me + far - step, [gate_on])
            up_back = part(up_set, me - far + step, [up_back])
        if step < near:
            up_on = part(up_set, me + near - step, [up_on])
            gate_back = part(gate_set, me - near + step, [gate_back])
        if step == near:
            gate_on, hidden_grad = lax.optimization_barrier((gate_on, hidden_grad))
    gate = part(gate_set, me, [gate_back, gate_on], F32)
    up = part(up_set, me, [up_on, up_back], F32)

    hidden_grad = hidden_grad.astype(F32)
    sig = jax.nn.sigmoid(gate)
    hidden = (gate * sig * up).astype(BF16)
    gate_delta = (hidden_grad * up * sig * (1.0 + gate * (1.0 - sig))).astype(BF16)
    up_delta = (hidden_grad * gate * sig).astype(BF16)

    hidden_t = lax.ppermute(hidden.T, ("row", "col"), meet_back)
    hidden_t = lax.all_gather(hidden_t, "col", axis=0, tiled=False)
    down_grad = down_grad_of(hidden_t, out_grad, down_wide, parts)

    gates, ups = {0: gate_delta}, {0: up_delta}
    gate_on = gate_back = gate_delta
    up_on = up_back = up_delta
    total = jnp.zeros((parts, tokens, depth), F32)
    inputs_t = jnp.swapaxes(inputs.reshape(parts, tokens, depth), 1, 2)

    def add(total, offset):
        return add_input_grad(
            where_is(me + offset), total, gates[offset % rows], ups[offset % rows],
            gate_weight, up_weight, gate_wide, up_wide,
        )

    total = add(total, 0)
    grads = None
    done = set()

    def column_cuts(grads):
        for j in range(cuts):
            offsets = [(j + cuts * i) % rows for i in range(parts)]
            if j not in done and all(o in gates and o in ups for o in offsets):
                done.add(j)
                at = jnp.stack([where_is(me + j)[1]] + [where_is(me + o)[0] for o in offsets])
                grads = weight_grads(
                    at, inputs_t, [gates[o] for o in offsets], [ups[o] for o in offsets],
                    gate_wide, up_wide, width, grads,
                )
        return grads

    for step in range(1, far + 1):
        gate_on, up_back = onward(gate_on), backward(up_back)
        gates[-step % rows], ups[step % rows] = gate_on, up_back
        if step <= near:
            up_on, gate_back = onward(up_on), backward(gate_back)
            ups[-step % rows], gates[step % rows] = up_on, gate_back
            total = add(total, -step)
            total = add(total, step)
            grads = column_cuts(grads)

    late = where_is(me - far)[0]
    others = [lax.rem(late + 1 + i, parts) for i in range(parts - 1)]
    early = [lax.dynamic_index_in_dim(total, o, 0, keepdims=False) for o in others]
    early = [sum_over_col(value, cols) for value in early]
    total = add(total, -far)
    grads = column_cuts(grads)
    last = sum_over_col(lax.dynamic_index_in_dim(total, late, 0, keepdims=False), cols)
    input_grad = jnp.zeros((parts, tokens, depth), BF16)
    for place_of, value in zip(others + [late], early + [last]):
        input_grad = lax.dynamic_update_index_in_dim(input_grad, value, place_of, 0)
    return (input_grad.reshape(count, depth), *grads, down_grad)


def sum_over_col(value, cols):
    half = value.shape[0] // 2
    mine = lax.axis_index("col") % 2

    def across(array, bit):
        return lax.ppermute(array, "col", [(c, c ^ bit) for c in range(cols)])

    other = lax.dynamic_slice_in_dim(value, (1 - mine) * half, half, 0)
    total = lax.dynamic_slice_in_dim(value, mine * half, half, 0) + across(other, 1)
    bit = 2
    while bit < cols:
        rounded = total.astype(BF16)
        total = rounded.astype(F32) + across(rounded, bit).astype(F32)
        bit *= 2
    own = total.astype(BF16)
    theirs = across(own, 1)
    first = mine == 0
    return jnp.concatenate([jnp.where(first, own, theirs), jnp.where(first, theirs, own)], axis=0)


def solution(mesh):
    placed = (P(None, "row"), P(None, "col")) + (P("row", "col"),) * 6
    return jax.shard_map(
        functools.partial(on_device, mesh.shape["row"], mesh.shape["col"]),
        mesh=mesh,
        in_specs=placed,
        out_specs=(P(None, "row"), P("row", "col"), P("row", "col"), P("row", "col")),
        check_vma=False,
    )
```

```python
import functools

import jax
import jax.numpy as jnp
from jax import lax
from jax.experimental import pallas as pl
from jax.experimental.pallas import tpu as pltpu
from jax.sharding import PartitionSpec as P

BLOCK = 128
ROWS = 16
BF16 = jnp.bfloat16
F32 = jnp.float32


def params(**more):
    return pltpu.CompilerParams(vmem_limit_bytes=50 * 1024 * 1024, **more)


def cost(flops, bytes_accessed):
    return pl.CostEstimate(flops=int(flops), bytes_accessed=int(bytes_accessed), transcendentals=0)


def widen(mask):
    return jnp.repeat(jnp.repeat(mask.astype(BF16), BLOCK, axis=1), ROWS, axis=0)


def masked(value, wide):
    rows, columns = value.shape
    blocks = rows // BLOCK
    spread = jnp.broadcast_to(
        wide.reshape(blocks, 1, ROWS, columns), (blocks, BLOCK // ROWS, ROWS, columns)
    )
    return value * spread.reshape(rows, columns)


def dot_nt(left, right):
    return lax.dot_general(left, right, (((1,), (1,)), ((), ())), preferred_element_type=F32)


def tile_of(size, most):
    best = BLOCK
    for tile in range(BLOCK, most + 1, BLOCK):
        if size % tile == 0:
            best = tile
    return best


def product_kernel(parts, at, x_ref, w_ref, m_ref, *outs):
    weight = masked(w_ref[...], m_ref[...])
    tokens = outs[0].shape[0]
    for i in range(parts):
        start = pl.multiple_of(at[1 + i] * tokens, tokens)
        term = jnp.dot(x_ref[pl.ds(start, tokens), :], weight, preferred_element_type=F32)
        outs[i][...] = term.astype(outs[i].dtype)


def products(at, inputs, weight, wide, columns, kinds):
    count, depth = inputs.shape
    parts = len(kinds)
    tokens = count // parts
    whole = pl.BlockSpec((tokens, columns), lambda k, at: (0, 0))
    return pl.pallas_call(
        functools.partial(product_kernel, parts),
        name="products",
        out_shape=tuple(jax.ShapeDtypeStruct((tokens, columns), kind) for kind in kinds),
        grid_spec=pltpu.PrefetchScalarGridSpec(
            num_scalar_prefetch=1,
            grid=(1,),
            in_specs=[
                pl.BlockSpec((count, depth), lambda k, at: (0, 0)),
                pl.BlockSpec((depth, columns), lambda k, at: (0, at[0])),
                pl.BlockSpec((wide.shape[0], columns), lambda k, at: (0, at[0])),
            ],
            out_specs=(whole,) * parts,
        ),
        compiler_params=params(),
        cost_estimate=cost(2 * count * depth * columns, 2 * depth * columns + 6 * count * columns),
    )(at, inputs, weight, wide)


def owner_kernel(gate_ref, gate_on, gate_back, up_ref, up_on, up_back, hg_ref, gd_ref, ud_ref, h_ref):
    gate = gate_ref[...] + gate_on[...].astype(F32) + gate_back[...].astype(F32)
    up = up_ref[...] + up_on[...].astype(F32) + up_back[...].astype(F32)
    hidden_grad = hg_ref[...].astype(F32)
    sig = jax.nn.sigmoid(gate)
    gated = gate * sig
    gd_ref[...] = (hidden_grad * up * sig * (1.0 + gate * (1.0 - sig))).astype(BF16)
    ud_ref[...] = (hidden_grad * gated).astype(BF16)
    h_ref[...] = (gated * up).T.astype(BF16)


def owner(*operands):
    tokens, columns = operands[0].shape
    tile = BLOCK
    block = pl.BlockSpec((tokens, tile), lambda i: (0, i))
    shape = jax.ShapeDtypeStruct((tokens, columns), BF16)
    return pl.pallas_call(
        owner_kernel,
        name="owner",
        out_shape=(shape, shape, jax.ShapeDtypeStruct((columns, tokens), BF16)),
        grid=(columns // tile,),
        in_specs=[block] * len(operands),
        out_specs=(block, block, pl.BlockSpec((tile, tokens), lambda i: (i, 0))),
        compiler_params=params(),
        cost_estimate=cost(0, 24 * tokens * columns),
    )(*operands)


def hidden_grad_kernel(at, g_ref, w_ref, m_ref, keep_ref, *send_refs):
    weight = masked(w_ref[...], m_ref[...])
    _, half, tokens, _ = keep_ref.shape

    def product(t):
        start = pl.multiple_of(t * tokens, tokens)
        return dot_nt(g_ref[pl.ds(start, tokens), :], weight)

    for t in range(half):
        keep_ref[0, t] = product(2 * t + at[0])
    for i, send_ref in enumerate(send_refs):

        @pl.when(pl.program_id(0) == i)
        def _():
            for t in range(half):
                send_ref[t] = product(2 * t + 1 - at[0]).astype(BF16)


def hidden_grad_partial(at, out_grad, weight, wide, parts, columns):
    count, depth = out_grad.shape
    cuts = weight.shape[0] // columns
    tokens = count // parts
    shape = (cuts, parts // 2, tokens, columns)
    keep = pl.BlockSpec((1,) + shape[1:], lambda i, at: (i, 0, 0, 0))
    send = pl.BlockSpec(shape[1:], lambda i, at: (0, 0, 0))
    return pl.pallas_call(
        hidden_grad_kernel,
        name="hidden_grad",
        out_shape=(jax.ShapeDtypeStruct(shape, F32),) + (jax.ShapeDtypeStruct(shape[1:], BF16),) * cuts,
        grid_spec=pltpu.PrefetchScalarGridSpec(
            num_scalar_prefetch=1,
            grid=(cuts,),
            in_specs=[
                pl.BlockSpec((count, depth), lambda i, at: (0, 0)),
                pl.BlockSpec((columns, depth), lambda i, at: (i, 0)),
                pl.BlockSpec((columns // BLOCK * ROWS, depth), lambda i, at: (i, 0)),
            ],
            out_specs=(keep,) + (send,) * cuts,
        ),
        compiler_params=params(),
        cost_estimate=cost(2 * count * depth * weight.shape[0], 2 * weight.size + 2 * out_grad.size + 4 * count * weight.shape[0]),
    )(at, out_grad, weight, wide)


def input_grad_kernel(at, sum_ref, gd_ref, ud_ref, gw_ref, uw_ref, gm_ref, um_ref, out_ref):
    term = dot_nt(gd_ref[...], masked(gw_ref[...], gm_ref[...]))
    term = term + dot_nt(ud_ref[...], masked(uw_ref[...], um_ref[...]))
    out_ref[0] = sum_ref[0] + term


def add_input_grad(at, total, gate_delta, up_delta, gate_weight, up_weight, gate_wide, up_wide):
    tokens, columns = gate_delta.shape
    depth = gate_weight.shape[0]
    tile = tile_of(depth, 512)
    delta = pl.BlockSpec((tokens, columns), lambda n, at: (0, 0))
    weight = pl.BlockSpec((tile, columns), lambda n, at: (n, at[1]))
    wide = pl.BlockSpec((tile // BLOCK * ROWS, columns), lambda n, at: (n, at[1]))
    sums = pl.BlockSpec((1, tokens, tile), lambda n, at: (at[0], 0, n))
    return pl.pallas_call(
        input_grad_kernel,
        name="input_grad",
        out_shape=jax.ShapeDtypeStruct(total.shape, F32),
        grid_spec=pltpu.PrefetchScalarGridSpec(
            num_scalar_prefetch=1,
            grid=(depth // tile,),
            in_specs=[sums, delta, delta, weight, weight, wide, wide],
            out_specs=sums,
        ),
        input_output_aliases={1: 0},
        compiler_params=params(),
        cost_estimate=cost(4 * tokens * depth * columns, 4 * depth * columns + 8 * tokens * depth),
    )(at, total, gate_delta, up_delta, gate_weight, up_weight, gate_wide, up_wide)


def weight_grads_kernel(parts, at, *refs):
    lefts, gates, ups = refs[:parts], refs[parts : 2 * parts], refs[2 * parts : 3 * parts]
    gm_ref, um_ref, gate_ref, up_ref = refs[3 * parts], refs[3 * parts + 1], refs[-2], refs[-1]
    for deltas, m_ref, out_ref in ((gates, gm_ref, gate_ref), (ups, um_ref, up_ref)):
        total = None
        for left, delta in zip(lefts, deltas):
            term = jnp.dot(left[0], delta[...], preferred_element_type=F32)
            total = term if total is None else total + term
        out_ref[...] = masked(total.astype(BF16), m_ref[...])


def weight_grads(at, inputs_t, gates, ups, gate_wide, up_wide, width, before):
    _, depth, tokens = inputs_t.shape
    parts, columns = len(gates), gates[0].shape[1]
    tile = tile_of(depth, 256)
    lefts = [
        pl.BlockSpec((1, tile, tokens), lambda m, at, i=i: (at[1 + i], m, 0)) for i in range(parts)
    ]
    delta = pl.BlockSpec((tokens, columns), lambda m, at: (0, 0))
    wide = pl.BlockSpec((tile // BLOCK * ROWS, columns), lambda m, at: (m, at[0]))
    out = pl.BlockSpec((tile, columns), lambda m, at: (m, at[0]))
    shape = jax.ShapeDtypeStruct((depth, width), BF16)
    operands = [inputs_t] * parts + gates + ups + [gate_wide, up_wide]
    specs = lefts + [delta] * (2 * parts) + [wide, wide]
    aliases = {}
    if before is not None:
        aliases = {1 + len(operands): 0, 2 + len(operands): 1}
        operands = operands + list(before)
        specs = specs + [pl.BlockSpec(memory_space=pl.ANY)] * 2
    return pl.pallas_call(
        functools.partial(weight_grads_kernel, parts),
        name="weight_grads",
        out_shape=(shape, shape),
        grid_spec=pltpu.PrefetchScalarGridSpec(
            num_scalar_prefetch=1,
            grid=(depth // tile,),
            in_specs=specs,
            out_specs=(out, out),
        ),
        input_output_aliases=aliases,
        compiler_params=params(),
        cost_estimate=cost(4 * parts * tokens * depth * columns, 4 * depth * columns + 4 * parts * tokens * columns),
    )(at, *operands)


def down_grad_kernel(parts, at, *refs):
    hiddens, grads, m_ref, out_ref = refs[:parts], refs[parts : 2 * parts], refs[2 * parts], refs[-1]
    total = None
    for hidden, grad in zip(hiddens, grads):
        term = jnp.dot(hidden[...], grad[0], preferred_element_type=F32)
        total = term if total is None else total + term
    out_ref[...] = masked(total.astype(BF16), m_ref[...])


def down_grad_cut(at, hiddens, out_grad, wide, before):
    parts = len(hiddens)
    columns, tokens = hiddens[0].shape
    width = out_grad.shape[2]
    tile = tile_of(width, 512)
    operands = list(hiddens) + [out_grad] * parts + [wide]
    specs = [pl.BlockSpec((columns, tokens), lambda j, at: (0, 0))] * parts
    specs += [
        pl.BlockSpec((1, tokens, tile), lambda j, at, i=i: (at[1 + i], 0, j)) for i in range(parts)
    ]
    specs += [pl.BlockSpec((columns // BLOCK * ROWS, tile), lambda j, at: (at[0], j))]
    aliases = {}
    if before is not None:
        aliases = {1 + len(operands): 0}
        operands.append(before)
        specs.append(pl.BlockSpec(memory_space=pl.ANY))
    return pl.pallas_call(
        functools.partial(down_grad_kernel, parts),
        name="down_grad",
        out_shape=jax.ShapeDtypeStruct((wide.shape[0] // ROWS * BLOCK, width), BF16),
        grid_spec=pltpu.PrefetchScalarGridSpec(
            num_scalar_prefetch=1,
            grid=(width // tile,),
            in_specs=specs,
            out_specs=pl.BlockSpec((columns, tile), lambda j, at: (at[0], j)),
        ),
        input_output_aliases=aliases,
        compiler_params=params(),
        cost_estimate=cost(2 * parts * tokens * columns * width, 2 * columns * width + 2 * out_grad.size),
    )(at, *operands)


def on_device(rows, cols, inputs, out_grad, gate_weight, up_weight, down_weight, gate_mask, up_mask, down_mask):
    count, depth = inputs.shape
    width = gate_weight.shape[1]
    ratio = rows // cols

    lines = rows // 4 if rows % 4 == 0 else 1
    length = rows // lines
    ring = []
    for line in range(lines):
        steps = range(length) if line % 2 == 0 else range(length - 1, -1, -1)
        ring += [step * lines + line for step in steps]
    place = [ring.index(r) for r in range(rows)]
    ahead = [(ring[p], ring[(p + 1) % rows]) for p in range(rows)]
    back = [(b, a) for a, b in ahead]
    me = jnp.array(place, jnp.int32)[lax.axis_index("row")]

    cuts = max(
        q for q in range(ratio, rows // 2 + 1, ratio) if rows % q == 0 and width // BLOCK % q == 0
    )
    parts = rows // cuts
    tokens, columns = count // parts, width // cuts
    far, near = rows // 2, rows - 1 - rows // 2

    def where_is(shard):
        shard = lax.rem(shard + 2 * rows, rows)
        return jnp.stack([shard // cuts, lax.rem(shard, cuts)])

    meet = []
    for r in range(rows):
        for c in range(cols):
            shard = (c % parts) * cuts + r % ratio * (cuts // ratio) + c // parts
            meet.append((r * cols + c, ring[shard] * cols + r // ratio))
    meet_back = [(b, a) for a, b in meet]

    gate_wide, up_wide, down_wide = widen(gate_mask), widen(up_mask), widen(down_mask)
    def onward(value):
        return lax.ppermute(value, "row", ahead)

    def backward(value):
        return lax.ppermute(value, "row", back)

    col = lax.axis_index("col")

    def across(array, bit):
        return lax.ppermute(array, "col", [(c, c ^ bit) for c in range(cols)])

    terms = {}

    def term(which, offset, kind=F32):
        offset %= rows
        if (which, offset) not in terms:
            weight, wide = {"gate": (gate_weight, gate_wide), "up": (up_weight, up_wide)}[which]
            offsets = [(offset + cuts * i) % rows for i in range(parts)]
            at = jnp.stack([where_is(me + offset)[1]] + [where_is(me + o)[0] for o in offsets])
            kinds = [kind] + [F32] * (parts - 1)
            values = products(at, inputs, weight, wide, columns, kinds)
            terms.update({(which, o): value for o, value in zip(offsets, values)})
        return terms[which, offset]

    def plus(which, offset, came):
        return (term(which, offset) + came.astype(F32)).astype(BF16)

    gate_on, up_back = term("gate", far, BF16), term("up", -far, BF16)
    up_on, gate_back = term("up", near, BF16), term("gate", -near, BF16)

    def hidden_grad_of(out_grad):
        held, *sent = hidden_grad_partial((col % 2)[None], out_grad, down_weight, down_wide, parts, columns)
        held = held + jnp.stack([across(value, 1) for value in sent]).astype(F32)
        bit = 2
        while bit < cols:
            held = held.reshape(-1, 2, tokens, columns)
            mine = col // bit % 2
            sent = lax.dynamic_index_in_dim(held, 1 - mine, 1, keepdims=False).astype(BF16)
            held = lax.dynamic_index_in_dim(held, mine, 1, keepdims=False) + across(sent, bit).astype(F32)
            bit *= 2
        return lax.ppermute(held.reshape(tokens, columns).astype(BF16), ("row", "col"), meet)

    for step in range(1, far + 1):
        gate_on, up_back = onward(gate_on), backward(up_back)
        if step <= near:
            up_on, gate_back = onward(up_on), backward(gate_back)
        if step == 1:
            out_grad, gate_on, up_back = lax.optimization_barrier((out_grad, gate_on, up_back))
            hidden_grad = hidden_grad_of(out_grad)
        if step < far:
            gate_on = plus("gate", far - step, gate_on)
            up_back = plus("up", step - far, up_back)
        if step < near:
            up_on = plus("up", near - step, up_on)
            gate_back = plus("gate", step - near, gate_back)
    gate_delta, up_delta, hidden_t = owner(
        term("gate", 0), gate_on, gate_back, term("up", 0), up_on, up_back, hidden_grad
    )

    hiddens = {0: lax.ppermute(hidden_t, ("row", "col"), meet_back)}
    bit = cols // 2
    while bit:
        hiddens.update({r ^ bit: across(value, bit) for r, value in list(hiddens.items())})
        bit //= 2
    grad_parts = out_grad.reshape(parts, tokens, -1)
    down_grad = None
    for cut in range(cols // parts):
        at = jnp.stack([(col // parts) ^ cut] + [(col % parts) ^ i for i in range(parts)])
        pieces = [hiddens[cut * parts + i] for i in range(parts)]
        down_grad = down_grad_cut(at, pieces, grad_parts, down_wide, down_grad)

    gates, ups = {0: gate_delta}, {0: up_delta}
    gate_on = gate_back = gate_delta
    up_on = up_back = up_delta
    total = jnp.zeros((parts, tokens, depth), F32)
    inputs_t = jnp.swapaxes(inputs.reshape(parts, tokens, depth), 1, 2)

    def add(total, offset):
        return add_input_grad(
            where_is(me + offset), total, gates[offset % rows], ups[offset % rows],
            gate_weight, up_weight, gate_wide, up_wide,
        )

    total = add(total, 0)
    grads = None
    done = set()

    def column_cuts(grads):
        for j in range(cuts):
            offsets = [(j + cuts * i) % rows for i in range(parts)]
            if j not in done and all(o in gates and o in ups for o in offsets):
                done.add(j)
                at = jnp.stack([where_is(me + j)[1]] + [where_is(me + o)[0] for o in offsets])
                grads = weight_grads(
                    at, inputs_t, [gates[o] for o in offsets], [ups[o] for o in offsets],
                    gate_wide, up_wide, width, grads,
                )
        return grads

    for step in range(1, far + 1):
        if step == far:
            gate_on, total, grads = lax.optimization_barrier((gate_on, total, grads))
        elif step > 1:
            up_on, total = lax.optimization_barrier((up_on, total))
        if step > 1:
            total = add(add(total, 1 - step), step - 1)
            grads = column_cuts(grads)
        gate_on, up_back = onward(gate_on), backward(up_back)
        gates[-step % rows], ups[step % rows] = gate_on, up_back
        if step <= near:
            up_on, gate_back = onward(up_on), backward(gate_back)
            ups[-step % rows], gates[step % rows] = up_on, gate_back

    total, gates[-far % rows], ups[far] = lax.optimization_barrier((total, gates[-far % rows], ups[far]))
    late = where_is(me - far)[0]
    others = [lax.rem(late + 1 + i, parts) for i in range(parts - 1)]
    early = [lax.dynamic_index_in_dim(total, o, 0, keepdims=False) for o in others]
    early = [sum_over_col(value, cols) for value in early]
    total = add(total, -far)
    grads = column_cuts(grads)
    last = sum_over_col(lax.dynamic_index_in_dim(total, late, 0, keepdims=False), cols)
    input_grad = jnp.zeros((parts, tokens, depth), BF16)
    for place_of, value in zip(others + [late], early + [last]):
        input_grad = lax.dynamic_update_index_in_dim(input_grad, value, place_of, 0)
    return (input_grad.reshape(count, depth), *grads, down_grad)


def sum_over_col(value, cols):
    half = value.shape[0] // 2
    mine = lax.axis_index("col") % 2

    def across(array, bit):
        return lax.ppermute(array, "col", [(c, c ^ bit) for c in range(cols)])

    other = lax.dynamic_slice_in_dim(value, (1 - mine) * half, half, 0)
    total = lax.dynamic_slice_in_dim(value, mine * half, half, 0) + across(other, 1)
    bit = 2
    while bit < cols:
        rounded = total.astype(BF16)
        total = rounded.astype(F32) + across(rounded, bit).astype(F32)
        bit *= 2
    own = total.astype(BF16)
    theirs = across(own, 1)
    first = mine == 0
    return jnp.concatenate([jnp.where(first, own, theirs), jnp.where(first, theirs, own)], axis=0)


def solution(mesh):
    placed = (P(None, "row"), P(None, "col")) + (P("row", "col"),) * 6
    return jax.shard_map(
        functools.partial(on_device, mesh.shape["row"], mesh.shape["col"]),
        mesh=mesh,
        in_specs=placed,
        out_specs=(P(None, "row"), P("row", "col"), P("row", "col"), P("row", "col")),
        check_vma=False,
    )
```

```python
import functools

import jax
import jax.numpy as jnp
from jax import lax
from jax.experimental import pallas as pl
from jax.experimental.pallas import tpu as pltpu
from jax.sharding import PartitionSpec as P

BLOCK = 128
ROWS = 16
BF16 = jnp.bfloat16
F32 = jnp.float32


def params(**more):
    return pltpu.CompilerParams(vmem_limit_bytes=50 * 1024 * 1024, **more)


def cost(flops, bytes_accessed):
    return pl.CostEstimate(flops=int(flops), bytes_accessed=int(bytes_accessed), transcendentals=0)


def widen(mask):
    return jnp.repeat(jnp.repeat(mask.astype(BF16), BLOCK, axis=1), ROWS, axis=0)


def masked(value, wide):
    rows, columns = value.shape
    blocks = rows // BLOCK
    spread = jnp.broadcast_to(
        wide.reshape(blocks, 1, ROWS, columns), (blocks, BLOCK // ROWS, ROWS, columns)
    )
    return value * spread.reshape(rows, columns)


def dot_nt(left, right):
    return lax.dot_general(left, right, (((1,), (1,)), ((), ())), preferred_element_type=F32)


def tile_of(size, most):
    best = BLOCK
    for tile in range(BLOCK, most + 1, BLOCK):
        if size % tile == 0:
            best = tile
    return best


def product_kernel(parts, at, x_ref, w_ref, m_ref, *outs):
    weight = masked(w_ref[...], m_ref[...])
    tokens = outs[0].shape[0]
    for i in range(parts):
        start = pl.multiple_of(at[1 + i] * tokens, tokens)
        term = jnp.dot(x_ref[pl.ds(start, tokens), :], weight, preferred_element_type=F32)
        outs[i][...] = term.astype(outs[i].dtype)


def products(at, inputs, weight, wide, columns, kinds):
    count, depth = inputs.shape
    parts = len(kinds)
    tokens = count // parts
    whole = pl.BlockSpec((tokens, columns), lambda k, at: (0, 0))
    return pl.pallas_call(
        functools.partial(product_kernel, parts),
        name="products",
        out_shape=tuple(jax.ShapeDtypeStruct((tokens, columns), kind) for kind in kinds),
        grid_spec=pltpu.PrefetchScalarGridSpec(
            num_scalar_prefetch=1,
            grid=(1,),
            in_specs=[
                pl.BlockSpec((count, depth), lambda k, at: (0, 0)),
                pl.BlockSpec((depth, columns), lambda k, at: (0, at[0])),
                pl.BlockSpec((wide.shape[0], columns), lambda k, at: (0, at[0])),
            ],
            out_specs=(whole,) * parts,
        ),
        compiler_params=params(),
        cost_estimate=cost(2 * count * depth * columns, 2 * depth * columns + 6 * count * columns),
    )(at, inputs, weight, wide)


def owner_kernel(gate_ref, gate_on, gate_back, up_ref, up_on, up_back, hg_ref, gd_ref, ud_ref, h_ref):
    gate = gate_ref[...] + gate_on[...].astype(F32) + gate_back[...].astype(F32)
    up = up_ref[...] + up_on[...].astype(F32) + up_back[...].astype(F32)
    hidden_grad = hg_ref[...].astype(F32)
    sig = jax.nn.sigmoid(gate)
    gated = gate * sig
    gd_ref[...] = (hidden_grad * up * sig * (1.0 + gate * (1.0 - sig))).astype(BF16)
    ud_ref[...] = (hidden_grad * gated).astype(BF16)
    h_ref[...] = (gated * up).T.astype(BF16)


def owner(*operands):
    tokens, columns = operands[0].shape
    tile = BLOCK
    block = pl.BlockSpec((tokens, tile), lambda i: (0, i))
    shape = jax.ShapeDtypeStruct((tokens, columns), BF16)
    return pl.pallas_call(
        owner_kernel,
        name="owner",
        out_shape=(shape, shape, jax.ShapeDtypeStruct((columns, tokens), BF16)),
        grid=(columns // tile,),
        in_specs=[block] * len(operands),
        out_specs=(block, block, pl.BlockSpec((tile, tokens), lambda i: (i, 0))),
        compiler_params=params(),
        cost_estimate=cost(0, 24 * tokens * columns),
    )(*operands)


def hidden_grad_kernel(at, g_ref, w_ref, m_ref, keep_ref, *send_refs):
    weight = masked(w_ref[...], m_ref[...])
    _, half, tokens, _ = keep_ref.shape

    def product(t):
        start = pl.multiple_of(t * tokens, tokens)
        return dot_nt(g_ref[pl.ds(start, tokens), :], weight)

    for t in range(half):
        keep_ref[0, t] = product(2 * t + at[0])
    for i, send_ref in enumerate(send_refs):

        @pl.when(pl.program_id(0) == i)
        def _():
            for t in range(half):
                send_ref[t] = product(2 * t + 1 - at[0]).astype(BF16)


def hidden_grad_partial(at, out_grad, weight, wide, parts, columns):
    count, depth = out_grad.shape
    cuts = weight.shape[0] // columns
    tokens = count // parts
    shape = (cuts, parts // 2, tokens, columns)
    keep = pl.BlockSpec((1,) + shape[1:], lambda i, at: (i, 0, 0, 0))
    send = pl.BlockSpec(shape[1:], lambda i, at: (0, 0, 0))
    return pl.pallas_call(
        hidden_grad_kernel,
        name="hidden_grad",
        out_shape=(jax.ShapeDtypeStruct(shape, F32),) + (jax.ShapeDtypeStruct(shape[1:], BF16),) * cuts,
        grid_spec=pltpu.PrefetchScalarGridSpec(
            num_scalar_prefetch=1,
            grid=(cuts,),
            in_specs=[
                pl.BlockSpec((count, depth), lambda i, at: (0, 0)),
                pl.BlockSpec((columns, depth), lambda i, at: (i, 0)),
                pl.BlockSpec((columns // BLOCK * ROWS, depth), lambda i, at: (i, 0)),
            ],
            out_specs=(keep,) + (send,) * cuts,
        ),
        compiler_params=params(),
        cost_estimate=cost(2 * count * depth * weight.shape[0], 2 * weight.size + 2 * out_grad.size + 4 * count * weight.shape[0]),
    )(at, out_grad, weight, wide)


def input_grad_kernel(at, sum_ref, gd_ref, ud_ref, gw_ref, uw_ref, gm_ref, um_ref, out_ref):
    term = dot_nt(gd_ref[...], masked(gw_ref[...], gm_ref[...]))
    term = term + dot_nt(ud_ref[...], masked(uw_ref[...], um_ref[...]))
    out_ref[0] = sum_ref[0] + term


def add_input_grad(at, total, gate_delta, up_delta, gate_weight, up_weight, gate_wide, up_wide):
    tokens, columns = gate_delta.shape
    depth = gate_weight.shape[0]
    tile = tile_of(depth, 512)
    delta = pl.BlockSpec((tokens, columns), lambda n, at: (0, 0))
    weight = pl.BlockSpec((tile, columns), lambda n, at: (n, at[1]))
    wide = pl.BlockSpec((tile // BLOCK * ROWS, columns), lambda n, at: (n, at[1]))
    sums = pl.BlockSpec((1, tokens, tile), lambda n, at: (at[0], 0, n))
    return pl.pallas_call(
        input_grad_kernel,
        name="input_grad",
        out_shape=jax.ShapeDtypeStruct(total.shape, F32),
        grid_spec=pltpu.PrefetchScalarGridSpec(
            num_scalar_prefetch=1,
            grid=(depth // tile,),
            in_specs=[sums, delta, delta, weight, weight, wide, wide],
            out_specs=sums,
        ),
        input_output_aliases={1: 0},
        compiler_params=params(),
        cost_estimate=cost(4 * tokens * depth * columns, 4 * depth * columns + 8 * tokens * depth),
    )(at, total, gate_delta, up_delta, gate_weight, up_weight, gate_wide, up_wide)


def weight_grads_kernel(parts, at, *refs):
    lefts, gates, ups = refs[:parts], refs[parts : 2 * parts], refs[2 * parts : 3 * parts]
    gm_ref, um_ref, gate_ref, up_ref = refs[3 * parts], refs[3 * parts + 1], refs[-2], refs[-1]
    for deltas, m_ref, out_ref in ((gates, gm_ref, gate_ref), (ups, um_ref, up_ref)):
        total = None
        for left, delta in zip(lefts, deltas):
            term = jnp.dot(left[0], delta[...], preferred_element_type=F32)
            total = term if total is None else total + term
        out_ref[...] = masked(total.astype(BF16), m_ref[...])


def weight_grads(at, inputs_t, gates, ups, gate_wide, up_wide, width, before):
    _, depth, tokens = inputs_t.shape
    parts, columns = len(gates), gates[0].shape[1]
    tile = tile_of(depth, 256)
    lefts = [
        pl.BlockSpec((1, tile, tokens), lambda m, at, i=i: (at[1 + i], m, 0)) for i in range(parts)
    ]
    delta = pl.BlockSpec((tokens, columns), lambda m, at: (0, 0))
    wide = pl.BlockSpec((tile // BLOCK * ROWS, columns), lambda m, at: (m, at[0]))
    out = pl.BlockSpec((tile, columns), lambda m, at: (m, at[0]))
    shape = jax.ShapeDtypeStruct((depth, width), BF16)
    operands = [inputs_t] * parts + gates + ups + [gate_wide, up_wide]
    specs = lefts + [delta] * (2 * parts) + [wide, wide]
    aliases = {}
    if before is not None:
        aliases = {1 + len(operands): 0, 2 + len(operands): 1}
        operands = operands + list(before)
        specs = specs + [pl.BlockSpec(memory_space=pl.ANY)] * 2
    return pl.pallas_call(
        functools.partial(weight_grads_kernel, parts),
        name="weight_grads",
        out_shape=(shape, shape),
        grid_spec=pltpu.PrefetchScalarGridSpec(
            num_scalar_prefetch=1,
            grid=(depth // tile,),
            in_specs=specs,
            out_specs=(out, out),
        ),
        input_output_aliases=aliases,
        compiler_params=params(),
        cost_estimate=cost(4 * parts * tokens * depth * columns, 4 * depth * columns + 4 * parts * tokens * columns),
    )(at, *operands)


def down_grad_kernel(parts, at, *refs):
    hiddens, grads, m_ref, out_ref = refs[:parts], refs[parts : 2 * parts], refs[2 * parts], refs[-1]
    total = None
    for hidden, grad in zip(hiddens, grads):
        term = jnp.dot(hidden[...], grad[0], preferred_element_type=F32)
        total = term if total is None else total + term
    out_ref[...] = masked(total.astype(BF16), m_ref[...])


def down_grad_cut(at, hiddens, out_grad, wide, before):
    parts = len(hiddens)
    columns, tokens = hiddens[0].shape
    width = out_grad.shape[2]
    tile = tile_of(width, 512)
    operands = list(hiddens) + [out_grad] * parts + [wide]
    specs = [pl.BlockSpec((columns, tokens), lambda j, at: (0, 0))] * parts
    specs += [
        pl.BlockSpec((1, tokens, tile), lambda j, at, i=i: (at[1 + i], 0, j)) for i in range(parts)
    ]
    specs += [pl.BlockSpec((columns // BLOCK * ROWS, tile), lambda j, at: (at[0], j))]
    aliases = {}
    if before is not None:
        aliases = {1 + len(operands): 0}
        operands.append(before)
        specs.append(pl.BlockSpec(memory_space=pl.ANY))
    return pl.pallas_call(
        functools.partial(down_grad_kernel, parts),
        name="down_grad",
        out_shape=jax.ShapeDtypeStruct((wide.shape[0] // ROWS * BLOCK, width), BF16),
        grid_spec=pltpu.PrefetchScalarGridSpec(
            num_scalar_prefetch=1,
            grid=(width // tile,),
            in_specs=specs,
            out_specs=pl.BlockSpec((columns, tile), lambda j, at: (at[0], j)),
        ),
        input_output_aliases=aliases,
        compiler_params=params(),
        cost_estimate=cost(2 * parts * tokens * columns * width, 2 * columns * width + 2 * out_grad.size),
    )(at, *operands)


def on_device(rows, cols, inputs, out_grad, gate_weight, up_weight, down_weight, gate_mask, up_mask, down_mask):
    count, depth = inputs.shape
    width = gate_weight.shape[1]
    ratio = rows // cols

    lines = rows // 4 if rows % 4 == 0 else 1
    length = rows // lines
    ring = []
    for line in range(lines):
        steps = range(length) if line % 2 == 0 else range(length - 1, -1, -1)
        ring += [step * lines + line for step in steps]
    place = [ring.index(r) for r in range(rows)]
    ahead = [(ring[p], ring[(p + 1) % rows]) for p in range(rows)]
    back = [(b, a) for a, b in ahead]
    turn = [(0, 1, 2, 0)[c % 4] for c in range(cols)]
    me = jnp.array(place, jnp.int32)[lax.axis_index("row")]
    me = lax.rem(me + jnp.array(turn, jnp.int32)[lax.axis_index("col")], rows)

    cuts = max(
        q for q in range(ratio, rows // 2 + 1, ratio) if rows % q == 0 and width // BLOCK % q == 0
    )
    parts = rows // cuts
    tokens, columns = count // parts, width // cuts
    far, near = rows // 2, rows - 1 - rows // 2

    def where_is(shard):
        shard = lax.rem(shard + 2 * rows, rows)
        return jnp.stack([shard // cuts, lax.rem(shard, cuts)])

    meet = []
    for r in range(rows):
        for c in range(cols):
            shard = (c % parts) * cuts + r % ratio * (cuts // ratio) + c // parts
            owner_row = ring[(shard - turn[r // ratio]) % rows]
            meet.append((r * cols + c, owner_row * cols + r // ratio))
    meet_back = [(b, a) for a, b in meet]

    gate_wide, up_wide, down_wide = widen(gate_mask), widen(up_mask), widen(down_mask)
    def onward(value):
        return lax.ppermute(value, "row", ahead)

    def backward(value):
        return lax.ppermute(value, "row", back)

    col = lax.axis_index("col")

    def across(array, bit):
        return lax.ppermute(array, "col", [(c, c ^ bit) for c in range(cols)])

    terms = {}

    def term(which, offset, kind=F32):
        offset %= rows
        if (which, offset) not in terms:
            weight, wide = {"gate": (gate_weight, gate_wide), "up": (up_weight, up_wide)}[which]
            offsets = [(offset + cuts * i) % rows for i in range(parts)]
            at = jnp.stack([where_is(me + offset)[1]] + [where_is(me + o)[0] for o in offsets])
            kinds = [kind] + [F32] * (parts - 1)
            values = products(at, inputs, weight, wide, columns, kinds)
            terms.update({(which, o): value for o, value in zip(offsets, values)})
        return terms[which, offset]

    def plus(which, offset, came):
        return (term(which, offset) + came.astype(F32)).astype(BF16)

    gate_on, up_back = term("gate", far, BF16), term("up", -far, BF16)
    up_on, gate_back = term("up", near, BF16), term("gate", -near, BF16)

    def hidden_grad_of(out_grad):
        held, *sent = hidden_grad_partial((col % 2)[None], out_grad, down_weight, down_wide, parts, columns)
        held = held + jnp.stack([across(value, 1) for value in sent]).astype(F32)
        bit = 2
        while bit < cols:
            held = held.reshape(-1, 2, tokens, columns)
            mine = col // bit % 2
            sent = lax.dynamic_index_in_dim(held, 1 - mine, 1, keepdims=False).astype(BF16)
            held = lax.dynamic_index_in_dim(held, mine, 1, keepdims=False) + across(sent, bit).astype(F32)
            bit *= 2
        return lax.ppermute(held.reshape(tokens, columns).astype(BF16), ("row", "col"), meet)

    for step in range(1, far + 1):
        gate_on, up_back = onward(gate_on), backward(up_back)
        if step <= near:
            up_on, gate_back = onward(up_on), backward(gate_back)
        if step == 1:
            out_grad, gate_on, up_back = lax.optimization_barrier((out_grad, gate_on, up_back))
            hidden_grad = hidden_grad_of(out_grad)
        if step < far:
            gate_on = plus("gate", far - step, gate_on)
            up_back = plus("up", step - far, up_back)
        if step < near:
            up_on = plus("up", near - step, up_on)
            gate_back = plus("gate", step - near, gate_back)
    gate_delta, up_delta, hidden_t = owner(
        term("gate", 0), gate_on, gate_back, term("up", 0), up_on, up_back, hidden_grad
    )

    hiddens = {0: lax.ppermute(hidden_t, ("row", "col"), meet_back)}
    bit = cols // 2
    while bit:
        hiddens.update({r ^ bit: across(value, bit) for r, value in list(hiddens.items())})
        bit //= 2
    grad_parts = out_grad.reshape(parts, tokens, -1)
    down_grad = None
    for cut in range(cols // parts):
        at = jnp.stack([(col // parts) ^ cut] + [(col % parts) ^ i for i in range(parts)])
        pieces = [hiddens[cut * parts + i] for i in range(parts)]
        down_grad = down_grad_cut(at, pieces, grad_parts, down_wide, down_grad)

    gates, ups = {0: gate_delta}, {0: up_delta}
    gate_on = gate_back = gate_delta
    up_on = up_back = up_delta
    total = jnp.zeros((parts, tokens, depth), F32)
    inputs_t = jnp.swapaxes(inputs.reshape(parts, tokens, depth), 1, 2)

    def add(total, offset):
        return add_input_grad(
            where_is(me + offset), total, gates[offset % rows], ups[offset % rows],
            gate_weight, up_weight, gate_wide, up_wide,
        )

    total = add(total, 0)
    grads = None
    done = set()

    def column_cuts(grads):
        for j in range(cuts):
            offsets = [(j + cuts * i) % rows for i in range(parts)]
            if j not in done and all(o in gates and o in ups for o in offsets):
                done.add(j)
                at = jnp.stack([where_is(me + j)[1]] + [where_is(me + o)[0] for o in offsets])
                grads = weight_grads(
                    at, inputs_t, [gates[o] for o in offsets], [ups[o] for o in offsets],
                    gate_wide, up_wide, width, grads,
                )
        return grads

    for step in range(1, far + 1):
        if step == far:
            gate_on, total, grads = lax.optimization_barrier((gate_on, total, grads))
        elif step > 1:
            up_on, total = lax.optimization_barrier((up_on, total))
        if step > 1:
            total = add(add(total, 1 - step), step - 1)
            grads = column_cuts(grads)
        gate_on, up_back = onward(gate_on), backward(up_back)
        gates[-step % rows], ups[step % rows] = gate_on, up_back
        if step <= near:
            up_on, gate_back = onward(up_on), backward(gate_back)
            ups[-step % rows], gates[step % rows] = up_on, gate_back

    total = add(total, -far)
    grads = column_cuts(grads)
    halves = [sum_over_col(value, cols) for value in jnp.split(total.reshape(count, depth), 2)]
    return (jnp.concatenate(halves), *grads, down_grad)


def sum_over_col(value, cols):
    half = value.shape[0] // 2
    mine = lax.axis_index("col") % 2

    def across(array, bit):
        return lax.ppermute(array, "col", [(c, c ^ bit) for c in range(cols)])

    other = lax.dynamic_slice_in_dim(value, (1 - mine) * half, half, 0)
    total = lax.dynamic_slice_in_dim(value, mine * half, half, 0) + across(other, 1)
    bit = 2
    while bit < cols:
        rounded = total.astype(BF16)
        total = rounded.astype(F32) + across(rounded, bit).astype(F32)
        bit *= 2
    own = total.astype(BF16)
    theirs = across(own, 1)
    first = mine == 0
    return jnp.concatenate([jnp.where(first, own, theirs), jnp.where(first, theirs, own)], axis=0)


def solution(mesh):
    placed = (P(None, "row"), P(None, "col")) + (P("row", "col"),) * 6
    return jax.shard_map(
        functools.partial(on_device, mesh.shape["row"], mesh.shape["col"]),
        mesh=mesh,
        in_specs=placed,
        out_specs=(P(None, "row"), P("row", "col"), P("row", "col"), P("row", "col")),
        check_vma=False,
    )
```

```python
import functools

import jax
import jax.numpy as jnp
from jax import lax
from jax.experimental import pallas as pl
from jax.experimental.pallas import tpu as pltpu
from jax.sharding import PartitionSpec as P

BLOCK = 128
ROWS = 16
BF16 = jnp.bfloat16
F32 = jnp.float32


def params(**more):
    return pltpu.CompilerParams(vmem_limit_bytes=50 * 1024 * 1024, **more)


def cost(flops, bytes_accessed):
    return pl.CostEstimate(flops=int(flops), bytes_accessed=int(bytes_accessed), transcendentals=0)


def widen(mask):
    return jnp.repeat(jnp.repeat(mask.astype(BF16), BLOCK, axis=1), ROWS, axis=0)


def masked(value, wide):
    rows, columns = value.shape
    blocks = rows // BLOCK
    spread = jnp.broadcast_to(
        wide.reshape(blocks, 1, ROWS, columns), (blocks, BLOCK // ROWS, ROWS, columns)
    )
    return value * spread.reshape(rows, columns)


def dot_nt(left, right):
    return lax.dot_general(left, right, (((1,), (1,)), ((), ())), preferred_element_type=F32)


def tile_of(size, most):
    best = BLOCK
    for tile in range(BLOCK, most + 1, BLOCK):
        if size % tile == 0:
            best = tile
    return best


def product_kernel(parts, at, x_ref, w_ref, m_ref, *outs):
    weight = masked(w_ref[...], m_ref[...])
    tokens = outs[0].shape[0]
    for i in range(parts):
        start = pl.multiple_of(at[1 + i] * tokens, tokens)
        term = jnp.dot(x_ref[pl.ds(start, tokens), :], weight, preferred_element_type=F32)
        outs[i][...] = term.astype(outs[i].dtype)


def products(at, inputs, weight, wide, columns, kinds):
    count, depth = inputs.shape
    parts = len(kinds)
    tokens = count // parts
    whole = pl.BlockSpec((tokens, columns), lambda k, at: (0, 0))
    return pl.pallas_call(
        functools.partial(product_kernel, parts),
        name="products",
        out_shape=tuple(jax.ShapeDtypeStruct((tokens, columns), kind) for kind in kinds),
        grid_spec=pltpu.PrefetchScalarGridSpec(
            num_scalar_prefetch=1,
            grid=(1,),
            in_specs=[
                pl.BlockSpec((count, depth), lambda k, at: (0, 0)),
                pl.BlockSpec((depth, columns), lambda k, at: (0, at[0])),
                pl.BlockSpec((wide.shape[0], columns), lambda k, at: (0, at[0])),
            ],
            out_specs=(whole,) * parts,
        ),
        compiler_params=params(),
        cost_estimate=cost(2 * count * depth * columns, 2 * depth * columns + 6 * count * columns),
    )(at, inputs, weight, wide)


def owner_kernel(gate_ref, gate_on, gate_back, up_ref, up_on, up_back, hg_ref, gd_ref, ud_ref, h_ref):
    gate = gate_ref[...] + gate_on[...].astype(F32) + gate_back[...].astype(F32)
    up = up_ref[...] + up_on[...].astype(F32) + up_back[...].astype(F32)
    hidden_grad = hg_ref[...].astype(F32)
    sig = jax.nn.sigmoid(gate)
    gated = gate * sig
    gd_ref[...] = (hidden_grad * up * sig * (1.0 + gate * (1.0 - sig))).astype(BF16)
    ud_ref[...] = (hidden_grad * gated).astype(BF16)
    h_ref[...] = (gated * up).T.astype(BF16)


def owner(*operands):
    tokens, columns = operands[0].shape
    tile = BLOCK
    block = pl.BlockSpec((tokens, tile), lambda i: (0, i))
    shape = jax.ShapeDtypeStruct((tokens, columns), BF16)
    return pl.pallas_call(
        owner_kernel,
        name="owner",
        out_shape=(shape, shape, jax.ShapeDtypeStruct((columns, tokens), BF16)),
        grid=(columns // tile,),
        in_specs=[block] * len(operands),
        out_specs=(block, block, pl.BlockSpec((tile, tokens), lambda i: (i, 0))),
        compiler_params=params(),
        cost_estimate=cost(0, 24 * tokens * columns),
    )(*operands)


def hidden_grad_kernel(at, g_ref, w_ref, m_ref, keep_ref, *send_refs):
    weight = masked(w_ref[...], m_ref[...])
    _, half, tokens, _ = keep_ref.shape

    def product(t):
        start = pl.multiple_of(t * tokens, tokens)
        return dot_nt(g_ref[pl.ds(start, tokens), :], weight)

    for t in range(half):
        keep_ref[0, t] = product(2 * t + at[0])
    for i, send_ref in enumerate(send_refs):

        @pl.when(pl.program_id(0) == i)
        def _():
            for t in range(half):
                send_ref[t] = product(2 * t + 1 - at[0]).astype(BF16)


def hidden_grad_partial(at, out_grad, weight, wide, parts, columns):
    count, depth = out_grad.shape
    cuts = weight.shape[0] // columns
    tokens = count // parts
    shape = (cuts, parts // 2, tokens, columns)
    keep = pl.BlockSpec((1,) + shape[1:], lambda i, at: (i, 0, 0, 0))
    send = pl.BlockSpec(shape[1:], lambda i, at: (0, 0, 0))
    return pl.pallas_call(
        hidden_grad_kernel,
        name="hidden_grad",
        out_shape=(jax.ShapeDtypeStruct(shape, F32),) + (jax.ShapeDtypeStruct(shape[1:], BF16),) * cuts,
        grid_spec=pltpu.PrefetchScalarGridSpec(
            num_scalar_prefetch=1,
            grid=(cuts,),
            in_specs=[
                pl.BlockSpec((count, depth), lambda i, at: (0, 0)),
                pl.BlockSpec((columns, depth), lambda i, at: (i, 0)),
                pl.BlockSpec((columns // BLOCK * ROWS, depth), lambda i, at: (i, 0)),
            ],
            out_specs=(keep,) + (send,) * cuts,
        ),
        compiler_params=params(),
        cost_estimate=cost(2 * count * depth * weight.shape[0], 2 * weight.size + 2 * out_grad.size + 4 * count * weight.shape[0]),
    )(at, out_grad, weight, wide)


def input_grad_kernel(at, sum_ref, gd_ref, ud_ref, gw_ref, uw_ref, gm_ref, um_ref, out_ref):
    term = dot_nt(gd_ref[...], masked(gw_ref[...], gm_ref[...]))
    term = term + dot_nt(ud_ref[...], masked(uw_ref[...], um_ref[...]))
    out_ref[0] = sum_ref[0] + term


def add_input_grad(at, total, gate_delta, up_delta, gate_weight, up_weight, gate_wide, up_wide):
    tokens, columns = gate_delta.shape
    depth = gate_weight.shape[0]
    tile = tile_of(depth, 512)
    delta = pl.BlockSpec((tokens, columns), lambda n, at: (0, 0))
    weight = pl.BlockSpec((tile, columns), lambda n, at: (n, at[1]))
    wide = pl.BlockSpec((tile // BLOCK * ROWS, columns), lambda n, at: (n, at[1]))
    sums = pl.BlockSpec((1, tokens, tile), lambda n, at: (at[0], 0, n))
    return pl.pallas_call(
        input_grad_kernel,
        name="input_grad",
        out_shape=jax.ShapeDtypeStruct(total.shape, F32),
        grid_spec=pltpu.PrefetchScalarGridSpec(
            num_scalar_prefetch=1,
            grid=(depth // tile,),
            in_specs=[sums, delta, delta, weight, weight, wide, wide],
            out_specs=sums,
        ),
        input_output_aliases={1: 0},
        compiler_params=params(),
        cost_estimate=cost(4 * tokens * depth * columns, 4 * depth * columns + 8 * tokens * depth),
    )(at, total, gate_delta, up_delta, gate_weight, up_weight, gate_wide, up_wide)


def weight_grads_kernel(parts, at, *refs):
    lefts, gates, ups = refs[:parts], refs[parts : 2 * parts], refs[2 * parts : 3 * parts]
    gm_ref, um_ref, gate_ref, up_ref = refs[3 * parts], refs[3 * parts + 1], refs[-2], refs[-1]
    for deltas, m_ref, out_ref in ((gates, gm_ref, gate_ref), (ups, um_ref, up_ref)):
        total = None
        for left, delta in zip(lefts, deltas):
            term = jnp.dot(left[0], delta[...], preferred_element_type=F32)
            total = term if total is None else total + term
        out_ref[...] = masked(total.astype(BF16), m_ref[...])


def weight_grads(at, inputs_t, gates, ups, gate_wide, up_wide, width, before):
    _, depth, tokens = inputs_t.shape
    parts, columns = len(gates), gates[0].shape[1]
    tile = tile_of(depth, 256)
    lefts = [
        pl.BlockSpec((1, tile, tokens), lambda m, at, i=i: (at[1 + i], m, 0)) for i in range(parts)
    ]
    delta = pl.BlockSpec((tokens, columns), lambda m, at: (0, 0))
    wide = pl.BlockSpec((tile // BLOCK * ROWS, columns), lambda m, at: (m, at[0]))
    out = pl.BlockSpec((tile, columns), lambda m, at: (m, at[0]))
    shape = jax.ShapeDtypeStruct((depth, width), BF16)
    operands = [inputs_t] * parts + gates + ups + [gate_wide, up_wide]
    specs = lefts + [delta] * (2 * parts) + [wide, wide]
    aliases = {}
    if before is not None:
        aliases = {1 + len(operands): 0, 2 + len(operands): 1}
        operands = operands + list(before)
        specs = specs + [pl.BlockSpec(memory_space=pl.ANY)] * 2
    return pl.pallas_call(
        functools.partial(weight_grads_kernel, parts),
        name="weight_grads",
        out_shape=(shape, shape),
        grid_spec=pltpu.PrefetchScalarGridSpec(
            num_scalar_prefetch=1,
            grid=(depth // tile,),
            in_specs=specs,
            out_specs=(out, out),
        ),
        input_output_aliases=aliases,
        compiler_params=params(),
        cost_estimate=cost(4 * parts * tokens * depth * columns, 4 * depth * columns + 4 * parts * tokens * columns),
    )(at, *operands)


def down_grad_kernel(parts, at, *refs):
    hiddens, grads, m_ref, out_ref = refs[:parts], refs[parts : 2 * parts], refs[2 * parts], refs[-1]
    total = None
    for hidden, grad in zip(hiddens, grads):
        term = jnp.dot(hidden[...], grad[0], preferred_element_type=F32)
        total = term if total is None else total + term
    out_ref[...] = masked(total.astype(BF16), m_ref[...])


def down_grad_cut(at, hiddens, out_grad, wide, before):
    parts = len(hiddens)
    columns, tokens = hiddens[0].shape
    width = out_grad.shape[2]
    tile = tile_of(width, 512)
    operands = list(hiddens) + [out_grad] * parts + [wide]
    specs = [pl.BlockSpec((columns, tokens), lambda j, at: (0, 0))] * parts
    specs += [
        pl.BlockSpec((1, tokens, tile), lambda j, at, i=i: (at[1 + i], 0, j)) for i in range(parts)
    ]
    specs += [pl.BlockSpec((columns // BLOCK * ROWS, tile), lambda j, at: (at[0], j))]
    aliases = {}
    if before is not None:
        aliases = {1 + len(operands): 0}
        operands.append(before)
        specs.append(pl.BlockSpec(memory_space=pl.ANY))
    return pl.pallas_call(
        functools.partial(down_grad_kernel, parts),
        name="down_grad",
        out_shape=jax.ShapeDtypeStruct((wide.shape[0] // ROWS * BLOCK, width), BF16),
        grid_spec=pltpu.PrefetchScalarGridSpec(
            num_scalar_prefetch=1,
            grid=(width // tile,),
            in_specs=specs,
            out_specs=pl.BlockSpec((columns, tile), lambda j, at: (at[0], j)),
        ),
        input_output_aliases=aliases,
        compiler_params=params(),
        cost_estimate=cost(2 * parts * tokens * columns * width, 2 * columns * width + 2 * out_grad.size),
    )(at, *operands)


def on_device(rows, cols, inputs, out_grad, gate_weight, up_weight, down_weight, gate_mask, up_mask, down_mask):
    count, depth = inputs.shape
    width = gate_weight.shape[1]
    ratio = rows // cols

    lines = rows // 4 if rows % 4 == 0 else 1
    length = rows // lines
    ring = []
    for line in range(lines):
        steps = range(length) if line % 2 == 0 else range(length - 1, -1, -1)
        ring += [step * lines + line for step in steps]
    place = [ring.index(r) for r in range(rows)]
    ahead = [(ring[p], ring[(p + 1) % rows]) for p in range(rows)]
    back = [(b, a) for a, b in ahead]
    turn = [(0, 2, 4, 6)[c % 4] for c in range(cols)]
    me = jnp.array(place, jnp.int32)[lax.axis_index("row")]
    me = lax.rem(me + jnp.array(turn, jnp.int32)[lax.axis_index("col")], rows)

    cuts = max(
        q for q in range(ratio, rows // 2 + 1, ratio) if rows % q == 0 and width // BLOCK % q == 0
    )
    parts = rows // cuts
    tokens, columns = count // parts, width // cuts
    far, near = rows // 2, rows - 1 - rows // 2

    def where_is(shard):
        shard = lax.rem(shard + 2 * rows, rows)
        return jnp.stack([shard // cuts, lax.rem(shard, cuts)])

    meet = []
    for r in range(rows):
        for c in range(cols):
            shard = (c % parts) * cuts + r % ratio * (cuts // ratio) + c // parts
            owner_row = ring[(shard - turn[r // ratio]) % rows]
            meet.append((r * cols + c, owner_row * cols + r // ratio))
    meet_back = [(b, a) for a, b in meet]

    gate_wide, up_wide, down_wide = widen(gate_mask), widen(up_mask), widen(down_mask)
    def onward(value):
        return lax.ppermute(value, "row", ahead)

    def backward(value):
        return lax.ppermute(value, "row", back)

    col = lax.axis_index("col")

    def across(array, bit):
        return lax.ppermute(array, "col", [(c, c ^ bit) for c in range(cols)])

    terms = {}

    def term(which, offset, kind=F32):
        offset %= rows
        if (which, offset) not in terms:
            weight, wide = {"gate": (gate_weight, gate_wide), "up": (up_weight, up_wide)}[which]
            offsets = [(offset + cuts * i) % rows for i in range(parts)]
            at = jnp.stack([where_is(me + offset)[1]] + [where_is(me + o)[0] for o in offsets])
            kinds = [kind] + [F32] * (parts - 1)
            values = products(at, inputs, weight, wide, columns, kinds)
            terms.update({(which, o): value for o, value in zip(offsets, values)})
        return terms[which, offset]

    def plus(which, offset, came):
        return (term(which, offset) + came.astype(F32)).astype(BF16)

    gate_on, up_back = term("gate", far, BF16), term("up", -far, BF16)
    up_on, gate_back = term("up", near, BF16), term("gate", -near, BF16)

    def hidden_grad_of(out_grad):
        held, *sent = hidden_grad_partial((col % 2)[None], out_grad, down_weight, down_wide, parts, columns)
        held = held + jnp.stack([across(value, 1) for value in sent]).astype(F32)
        bit = 2
        while bit < cols:
            held = held.reshape(-1, 2, tokens, columns)
            mine = col // bit % 2
            sent = lax.dynamic_index_in_dim(held, 1 - mine, 1, keepdims=False).astype(BF16)
            held = lax.dynamic_index_in_dim(held, mine, 1, keepdims=False) + across(sent, bit).astype(F32)
            bit *= 2
        return lax.ppermute(held.reshape(tokens, columns).astype(BF16), ("row", "col"), meet)

    for step in range(1, far + 1):
        gate_on, up_back = onward(gate_on), backward(up_back)
        if step <= near:
            up_on, gate_back = onward(up_on), backward(gate_back)
        if step == 1:
            out_grad, gate_on, up_back = lax.optimization_barrier((out_grad, gate_on, up_back))
            hidden_grad = hidden_grad_of(out_grad)
        if step < far:
            gate_on = plus("gate", far - step, gate_on)
            up_back = plus("up", step - far, up_back)
        if step < near:
            up_on = plus("up", near - step, up_on)
            gate_back = plus("gate", step - near, gate_back)
    gate_delta, up_delta, hidden_t = owner(
        term("gate", 0), gate_on, gate_back, term("up", 0), up_on, up_back, hidden_grad
    )

    hiddens = {0: lax.ppermute(hidden_t, ("row", "col"), meet_back)}
    bit = cols // 2
    while bit:
        hiddens.update({r ^ bit: across(value, bit) for r, value in list(hiddens.items())})
        bit //= 2
    grad_parts = out_grad.reshape(parts, tokens, -1)
    down_grad = None
    for cut in range(cols // parts):
        at = jnp.stack([(col // parts) ^ cut] + [(col % parts) ^ i for i in range(parts)])
        pieces = [hiddens[cut * parts + i] for i in range(parts)]
        down_grad = down_grad_cut(at, pieces, grad_parts, down_wide, down_grad)

    gates, ups = {0: gate_delta}, {0: up_delta}
    gate_on = gate_back = gate_delta
    up_on = up_back = up_delta
    total = jnp.zeros((parts, tokens, depth), F32)
    inputs_t = jnp.swapaxes(inputs.reshape(parts, tokens, depth), 1, 2)

    def add(total, offset):
        return add_input_grad(
            where_is(me + offset), total, gates[offset % rows], ups[offset % rows],
            gate_weight, up_weight, gate_wide, up_wide,
        )

    total = add(total, 0)
    grads = None
    done = set()

    def column_cuts(grads):
        for j in range(cuts):
            offsets = [(j + cuts * i) % rows for i in range(parts)]
            if j not in done and all(o in gates and o in ups for o in offsets):
                done.add(j)
                at = jnp.stack([where_is(me + j)[1]] + [where_is(me + o)[0] for o in offsets])
                grads = weight_grads(
                    at, inputs_t, [gates[o] for o in offsets], [ups[o] for o in offsets],
                    gate_wide, up_wide, width, grads,
                )
        return grads

    for step in range(1, far + 1):
        if step == far:
            gate_on, total, grads = lax.optimization_barrier((gate_on, total, grads))
        elif step > 1:
            up_on, total = lax.optimization_barrier((up_on, total))
        if step > 1:
            total = add(add(total, 1 - step), step - 1)
            grads = column_cuts(grads)
        gate_on, up_back = onward(gate_on), backward(up_back)
        gates[-step % rows], ups[step % rows] = gate_on, up_back
        if step <= near:
            up_on, gate_back = onward(up_on), backward(gate_back)
            ups[-step % rows], gates[step % rows] = up_on, gate_back

    total, grads = lax.optimization_barrier((total, grads))
    total = add(total, -far)
    grads = column_cuts(grads)
    halves = [sum_over_col(value, cols) for value in jnp.split(total.reshape(count, depth), 2)]
    return (jnp.concatenate(halves), *grads, down_grad)


def sum_over_col(value, cols):
    half = value.shape[0] // 2
    mine = lax.axis_index("col") % 2

    def across(array, bit):
        return lax.ppermute(array, "col", [(c, c ^ bit) for c in range(cols)])

    other = lax.dynamic_slice_in_dim(value, (1 - mine) * half, half, 0)
    total = lax.dynamic_slice_in_dim(value, mine * half, half, 0) + across(other, 1)
    bit = 2
    while bit < cols:
        rounded = total.astype(BF16)
        total = rounded.astype(F32) + across(rounded, bit).astype(F32)
        bit *= 2
    own = total.astype(BF16)
    theirs = across(own, 1)
    first = mine == 0
    return jnp.concatenate([jnp.where(first, own, theirs), jnp.where(first, theirs, own)], axis=0)


def solution(mesh):
    placed = (P(None, "row"), P(None, "col")) + (P("row", "col"),) * 6
    return jax.shard_map(
        functools.partial(on_device, mesh.shape["row"], mesh.shape["col"]),
        mesh=mesh,
        in_specs=placed,
        out_specs=(P(None, "row"), P("row", "col"), P("row", "col"), P("row", "col")),
        check_vma=False,
    )
```

```python
import functools

import jax
import jax.numpy as jnp
from jax import lax
from jax.experimental import pallas as pl
from jax.experimental.pallas import tpu as pltpu
from jax.sharding import PartitionSpec as P

BLOCK = 128
ROWS = 16
BF16 = jnp.bfloat16
F32 = jnp.float32


def params(**more):
    return pltpu.CompilerParams(vmem_limit_bytes=50 * 1024 * 1024, **more)


def cost(flops, bytes_accessed):
    return pl.CostEstimate(flops=int(flops), bytes_accessed=int(bytes_accessed), transcendentals=0)


def widen(mask):
    return jnp.repeat(jnp.repeat(mask.astype(BF16), BLOCK, axis=1), ROWS, axis=0)


def masked(value, wide):
    rows, columns = value.shape
    blocks = rows // BLOCK
    spread = jnp.broadcast_to(
        wide.reshape(blocks, 1, ROWS, columns), (blocks, BLOCK // ROWS, ROWS, columns)
    )
    return value * spread.reshape(rows, columns)


def dot_nt(left, right):
    return lax.dot_general(left, right, (((1,), (1,)), ((), ())), preferred_element_type=F32)


def tile_of(size, most):
    best = BLOCK
    for tile in range(BLOCK, most + 1, BLOCK):
        if size % tile == 0:
            best = tile
    return best


def product_kernel(parts, at, x_ref, w_ref, m_ref, *outs):
    weight = masked(w_ref[...], m_ref[...])
    tokens = outs[0].shape[0]
    for i in range(parts):
        start = pl.multiple_of(at[1 + i] * tokens, tokens)
        term = jnp.dot(x_ref[pl.ds(start, tokens), :], weight, preferred_element_type=F32)
        outs[i][...] = term.astype(outs[i].dtype)


def products(at, inputs, weight, wide, columns, kinds):
    count, depth = inputs.shape
    parts = len(kinds)
    tokens = count // parts
    whole = pl.BlockSpec((tokens, columns), lambda k, at: (0, 0))
    return pl.pallas_call(
        functools.partial(product_kernel, parts),
        name="products",
        out_shape=tuple(jax.ShapeDtypeStruct((tokens, columns), kind) for kind in kinds),
        grid_spec=pltpu.PrefetchScalarGridSpec(
            num_scalar_prefetch=1,
            grid=(1,),
            in_specs=[
                pl.BlockSpec((count, depth), lambda k, at: (0, 0)),
                pl.BlockSpec((depth, columns), lambda k, at: (0, at[0])),
                pl.BlockSpec((wide.shape[0], columns), lambda k, at: (0, at[0])),
            ],
            out_specs=(whole,) * parts,
        ),
        compiler_params=params(),
        cost_estimate=cost(2 * count * depth * columns, 2 * depth * columns + 6 * count * columns),
    )(at, inputs, weight, wide)


def owner_kernel(gate_ref, gate_on, gate_back, up_ref, up_on, up_back, hg_ref, gd_ref, ud_ref, h_ref):
    gate = gate_ref[...] + gate_on[...].astype(F32) + gate_back[...].astype(F32)
    up = up_ref[...] + up_on[...].astype(F32) + up_back[...].astype(F32)
    hidden_grad = hg_ref[...].astype(F32)
    sig = jax.nn.sigmoid(gate)
    gated = gate * sig
    gd_ref[...] = (hidden_grad * up * sig * (1.0 + gate * (1.0 - sig))).astype(BF16)
    ud_ref[...] = (hidden_grad * gated).astype(BF16)
    h_ref[...] = (gated * up).T.astype(BF16)


def owner(*operands):
    tokens, columns = operands[0].shape
    tile = BLOCK
    block = pl.BlockSpec((tokens, tile), lambda i: (0, i))
    shape = jax.ShapeDtypeStruct((tokens, columns), BF16)
    return pl.pallas_call(
        owner_kernel,
        name="owner",
        out_shape=(shape, shape, jax.ShapeDtypeStruct((columns, tokens), BF16)),
        grid=(columns // tile,),
        in_specs=[block] * len(operands),
        out_specs=(block, block, pl.BlockSpec((tile, tokens), lambda i: (i, 0))),
        compiler_params=params(),
        cost_estimate=cost(0, 24 * tokens * columns),
    )(*operands)


def hidden_grad_kernel(at, g_ref, w_ref, m_ref, keep_ref, *send_refs):
    weight = masked(w_ref[...], m_ref[...])
    _, half, tokens, _ = keep_ref.shape

    def product(t):
        start = pl.multiple_of(t * tokens, tokens)
        return dot_nt(g_ref[pl.ds(start, tokens), :], weight)

    for t in range(half):
        keep_ref[0, t] = product(2 * t + at[0])
    for i, send_ref in enumerate(send_refs):

        @pl.when(pl.program_id(0) == i)
        def _():
            for t in range(half):
                send_ref[t] = product(2 * t + 1 - at[0]).astype(BF16)


def hidden_grad_partial(at, out_grad, weight, wide, parts, columns):
    count, depth = out_grad.shape
    cuts = weight.shape[0] // columns
    tokens = count // parts
    shape = (cuts, parts // 2, tokens, columns)
    keep = pl.BlockSpec((1,) + shape[1:], lambda i, at: (i, 0, 0, 0))
    send = pl.BlockSpec(shape[1:], lambda i, at: (0, 0, 0))
    return pl.pallas_call(
        hidden_grad_kernel,
        name="hidden_grad",
        out_shape=(jax.ShapeDtypeStruct(shape, F32),) + (jax.ShapeDtypeStruct(shape[1:], BF16),) * cuts,
        grid_spec=pltpu.PrefetchScalarGridSpec(
            num_scalar_prefetch=1,
            grid=(cuts,),
            in_specs=[
                pl.BlockSpec((count, depth), lambda i, at: (0, 0)),
                pl.BlockSpec((columns, depth), lambda i, at: (i, 0)),
                pl.BlockSpec((columns // BLOCK * ROWS, depth), lambda i, at: (i, 0)),
            ],
            out_specs=(keep,) + (send,) * cuts,
        ),
        compiler_params=params(),
        cost_estimate=cost(2 * count * depth * weight.shape[0], 2 * weight.size + 2 * out_grad.size + 4 * count * weight.shape[0]),
    )(at, out_grad, weight, wide)


def input_grad_kernel(at, sum_ref, gd_ref, ud_ref, gw_ref, uw_ref, gm_ref, um_ref, out_ref):
    term = dot_nt(gd_ref[...], masked(gw_ref[...], gm_ref[...]))
    term = term + dot_nt(ud_ref[...], masked(uw_ref[...], um_ref[...]))
    out_ref[0] = sum_ref[0] + term


def add_input_grad(at, total, gate_delta, up_delta, gate_weight, up_weight, gate_wide, up_wide):
    tokens, columns = gate_delta.shape
    depth = gate_weight.shape[0]
    tile = tile_of(depth, 512)
    delta = pl.BlockSpec((tokens, columns), lambda n, at: (0, 0))
    weight = pl.BlockSpec((tile, columns), lambda n, at: (n, at[1]))
    wide = pl.BlockSpec((tile // BLOCK * ROWS, columns), lambda n, at: (n, at[1]))
    sums = pl.BlockSpec((1, tokens, tile), lambda n, at: (at[0], 0, n))
    return pl.pallas_call(
        input_grad_kernel,
        name="input_grad",
        out_shape=jax.ShapeDtypeStruct(total.shape, F32),
        grid_spec=pltpu.PrefetchScalarGridSpec(
            num_scalar_prefetch=1,
            grid=(depth // tile,),
            in_specs=[sums, delta, delta, weight, weight, wide, wide],
            out_specs=sums,
        ),
        input_output_aliases={1: 0},
        compiler_params=params(),
        cost_estimate=cost(4 * tokens * depth * columns, 4 * depth * columns + 8 * tokens * depth),
    )(at, total, gate_delta, up_delta, gate_weight, up_weight, gate_wide, up_wide)


def weight_grads_kernel(parts, at, *refs):
    lefts, gates, ups = refs[:parts], refs[parts : 2 * parts], refs[2 * parts : 3 * parts]
    gm_ref, um_ref, gate_ref, up_ref = refs[3 * parts], refs[3 * parts + 1], refs[-2], refs[-1]
    for deltas, m_ref, out_ref in ((gates, gm_ref, gate_ref), (ups, um_ref, up_ref)):
        total = None
        for left, delta in zip(lefts, deltas):
            term = jnp.dot(left[0], delta[...], preferred_element_type=F32)
            total = term if total is None else total + term
        out_ref[...] = masked(total.astype(BF16), m_ref[...])


def weight_grads(at, inputs_t, gates, ups, gate_wide, up_wide, width, before):
    _, depth, tokens = inputs_t.shape
    parts, columns = len(gates), gates[0].shape[1]
    tile = tile_of(depth, 256)
    lefts = [
        pl.BlockSpec((1, tile, tokens), lambda m, at, i=i: (at[1 + i], m, 0)) for i in range(parts)
    ]
    delta = pl.BlockSpec((tokens, columns), lambda m, at: (0, 0))
    wide = pl.BlockSpec((tile // BLOCK * ROWS, columns), lambda m, at: (m, at[0]))
    out = pl.BlockSpec((tile, columns), lambda m, at: (m, at[0]))
    shape = jax.ShapeDtypeStruct((depth, width), BF16)
    operands = [inputs_t] * parts + gates + ups + [gate_wide, up_wide]
    specs = lefts + [delta] * (2 * parts) + [wide, wide]
    aliases = {}
    if before is not None:
        aliases = {1 + len(operands): 0, 2 + len(operands): 1}
        operands = operands + list(before)
        specs = specs + [pl.BlockSpec(memory_space=pl.ANY)] * 2
    return pl.pallas_call(
        functools.partial(weight_grads_kernel, parts),
        name="weight_grads",
        out_shape=(shape, shape),
        grid_spec=pltpu.PrefetchScalarGridSpec(
            num_scalar_prefetch=1,
            grid=(depth // tile,),
            in_specs=specs,
            out_specs=(out, out),
        ),
        input_output_aliases=aliases,
        compiler_params=params(),
        cost_estimate=cost(4 * parts * tokens * depth * columns, 4 * depth * columns + 4 * parts * tokens * columns),
    )(at, *operands)


def down_grad_kernel(parts, at, *refs):
    hiddens, grads, m_ref, out_ref = refs[:parts], refs[parts : 2 * parts], refs[2 * parts], refs[-1]
    total = None
    for hidden, grad in zip(hiddens, grads):
        term = jnp.dot(hidden[...], grad[0], preferred_element_type=F32)
        total = term if total is None else total + term
    out_ref[...] = masked(total.astype(BF16), m_ref[...])


def down_grad_cut(at, hiddens, out_grad, wide, before):
    parts = len(hiddens)
    columns, tokens = hiddens[0].shape
    width = out_grad.shape[2]
    tile = tile_of(width, 512)
    operands = list(hiddens) + [out_grad] * parts + [wide]
    specs = [pl.BlockSpec((columns, tokens), lambda j, at: (0, 0))] * parts
    specs += [
        pl.BlockSpec((1, tokens, tile), lambda j, at, i=i: (at[1 + i], 0, j)) for i in range(parts)
    ]
    specs += [pl.BlockSpec((columns // BLOCK * ROWS, tile), lambda j, at: (at[0], j))]
    aliases = {}
    if before is not None:
        aliases = {1 + len(operands): 0}
        operands.append(before)
        specs.append(pl.BlockSpec(memory_space=pl.ANY))
    return pl.pallas_call(
        functools.partial(down_grad_kernel, parts),
        name="down_grad",
        out_shape=jax.ShapeDtypeStruct((wide.shape[0] // ROWS * BLOCK, width), BF16),
        grid_spec=pltpu.PrefetchScalarGridSpec(
            num_scalar_prefetch=1,
            grid=(width // tile,),
            in_specs=specs,
            out_specs=pl.BlockSpec((columns, tile), lambda j, at: (at[0], j)),
        ),
        input_output_aliases=aliases,
        compiler_params=params(),
        cost_estimate=cost(2 * parts * tokens * columns * width, 2 * columns * width + 2 * out_grad.size),
    )(at, *operands)


def on_device(rows, cols, inputs, out_grad, gate_weight, up_weight, down_weight, gate_mask, up_mask, down_mask):
    count, depth = inputs.shape
    width = gate_weight.shape[1]
    ratio = rows // cols

    lines = rows // 4 if rows % 4 == 0 else 1
    length = rows // lines
    ring = []
    for line in range(lines):
        steps = range(length) if line % 2 == 0 else range(length - 1, -1, -1)
        ring += [step * lines + line for step in steps]
    place = [ring.index(r) for r in range(rows)]
    ahead = [(ring[p], ring[(p + 1) % rows]) for p in range(rows)]
    back = [(b, a) for a, b in ahead]
    turn = [(0, 6, 4, 2)[c % 4] for c in range(cols)]
    me = jnp.array(place, jnp.int32)[lax.axis_index("row")]
    me = lax.rem(me + jnp.array(turn, jnp.int32)[lax.axis_index("col")], rows)

    cuts = max(
        q for q in range(ratio, rows // 2 + 1, ratio) if rows % q == 0 and width // BLOCK % q == 0
    )
    parts = rows // cuts
    tokens, columns = count // parts, width // cuts
    far, near = rows // 2, rows - 1 - rows // 2

    def where_is(shard):
        shard = lax.rem(shard + 2 * rows, rows)
        return jnp.stack([shard // cuts, lax.rem(shard, cuts)])

    meet = []
    for r in range(rows):
        for c in range(cols):
            shard = (c % parts) * cuts + r % ratio * (cuts // ratio) + c // parts
            owner_row = ring[(shard - turn[r // ratio]) % rows]
            meet.append((r * cols + c, owner_row * cols + r // ratio))
    meet_back = [(b, a) for a, b in meet]

    gate_wide, up_wide, down_wide = widen(gate_mask), widen(up_mask), widen(down_mask)
    def onward(value):
        return lax.ppermute(value, "row", ahead)

    def backward(value):
        return lax.ppermute(value, "row", back)

    col = lax.axis_index("col")

    def across(array, bit):
        return lax.ppermute(array, "col", [(c, c ^ bit) for c in range(cols)])

    terms = {}

    def term(which, offset, kind=F32):
        offset %= rows
        if (which, offset) not in terms:
            weight, wide = {"gate": (gate_weight, gate_wide), "up": (up_weight, up_wide)}[which]
            offsets = [(offset + cuts * i) % rows for i in range(parts)]
            at = jnp.stack([where_is(me + offset)[1]] + [where_is(me + o)[0] for o in offsets])
            kinds = [kind] + [F32] * (parts - 1)
            values = products(at, inputs, weight, wide, columns, kinds)
            terms.update({(which, o): value for o, value in zip(offsets, values)})
        return terms[which, offset]

    def plus(which, offset, came):
        return (term(which, offset) + came.astype(F32)).astype(BF16)

    gate_on, up_back = term("gate", far, BF16), term("up", -far, BF16)
    up_on, gate_back = term("up", near, BF16), term("gate", -near, BF16)

    def hidden_grad_of(out_grad):
        held, *sent = hidden_grad_partial((col % 2)[None], out_grad, down_weight, down_wide, parts, columns)
        held = held + jnp.stack([across(value, 1) for value in sent]).astype(F32)
        bit = 2
        while bit < cols:
            held = held.reshape(-1, 2, tokens, columns)
            mine = col // bit % 2
            sent = lax.dynamic_index_in_dim(held, 1 - mine, 1, keepdims=False).astype(BF16)
            held = lax.dynamic_index_in_dim(held, mine, 1, keepdims=False) + across(sent, bit).astype(F32)
            bit *= 2
        return lax.ppermute(held.reshape(tokens, columns).astype(BF16), ("row", "col"), meet)

    for step in range(1, far + 1):
        gate_on, up_back = onward(gate_on), backward(up_back)
        if step <= near:
            up_on, gate_back = onward(up_on), backward(gate_back)
        if step == 1:
            out_grad, gate_on, up_back = lax.optimization_barrier((out_grad, gate_on, up_back))
            hidden_grad = hidden_grad_of(out_grad)
        if step < far:
            gate_on = plus("gate", far - step, gate_on)
            up_back = plus("up", step - far, up_back)
        if step < near:
            up_on = plus("up", near - step, up_on)
            gate_back = plus("gate", step - near, gate_back)
    gate_delta, up_delta, hidden_t = owner(
        term("gate", 0), gate_on, gate_back, term("up", 0), up_on, up_back, hidden_grad
    )

    hiddens = {0: lax.ppermute(hidden_t, ("row", "col"), meet_back)}
    bit = cols // 2
    while bit:
        hiddens.update({r ^ bit: across(value, bit) for r, value in list(hiddens.items())})
        bit //= 2
    grad_parts = out_grad.reshape(parts, tokens, -1)
    down_grad = None
    for cut in range(cols // parts):
        at = jnp.stack([(col // parts) ^ cut] + [(col % parts) ^ i for i in range(parts)])
        pieces = [hiddens[cut * parts + i] for i in range(parts)]
        down_grad = down_grad_cut(at, pieces, grad_parts, down_wide, down_grad)

    gates, ups = {0: gate_delta}, {0: up_delta}
    gate_on = gate_back = gate_delta
    up_on = up_back = up_delta
    total = jnp.zeros((parts, tokens, depth), F32)
    inputs_t = jnp.swapaxes(inputs.reshape(parts, tokens, depth), 1, 2)

    def add(total, offset):
        return add_input_grad(
            where_is(me + offset), total, gates[offset % rows], ups[offset % rows],
            gate_weight, up_weight, gate_wide, up_wide,
        )

    total = add(total, 0)
    grads = None
    done = set()

    def column_cuts(grads):
        for j in range(cuts):
            offsets = [(j + cuts * i) % rows for i in range(parts)]
            if j not in done and all(o in gates and o in ups for o in offsets):
                done.add(j)
                at = jnp.stack([where_is(me + j)[1]] + [where_is(me + o)[0] for o in offsets])
                grads = weight_grads(
                    at, inputs_t, [gates[o] for o in offsets], [ups[o] for o in offsets],
                    gate_wide, up_wide, width, grads,
                )
        return grads

    for step in range(1, far + 1):
        if step == far:
            gate_on, total, grads = lax.optimization_barrier((gate_on, total, grads))
        elif step > 1:
            up_on, total = lax.optimization_barrier((up_on, total))
        if step > 1:
            total = add(add(total, 1 - step), step - 1)
            grads = column_cuts(grads)
        gate_on, up_back = onward(gate_on), backward(up_back)
        gates[-step % rows], ups[step % rows] = gate_on, up_back
        if step <= near:
            up_on, gate_back = onward(up_on), backward(gate_back)
            ups[-step % rows], gates[step % rows] = up_on, gate_back

    total, grads = lax.optimization_barrier((total, grads))
    total = add(total, -far)
    grads = column_cuts(grads)
    halves = [sum_over_col(value, cols) for value in jnp.split(total.reshape(count, depth), 2)]
    return (jnp.concatenate(halves), *grads, down_grad)


def sum_over_col(value, cols):
    half = value.shape[0] // 2
    mine = lax.axis_index("col") % 2

    def across(array, bit):
        return lax.ppermute(array, "col", [(c, c ^ bit) for c in range(cols)])

    other = lax.dynamic_slice_in_dim(value, (1 - mine) * half, half, 0)
    total = lax.dynamic_slice_in_dim(value, mine * half, half, 0) + across(other, 1)
    bit = 2
    while bit < cols:
        rounded = total.astype(BF16)
        total = rounded.astype(F32) + across(rounded, bit).astype(F32)
        bit *= 2
    own = total.astype(BF16)
    theirs = across(own, 1)
    first = mine == 0
    return jnp.concatenate([jnp.where(first, own, theirs), jnp.where(first, theirs, own)], axis=0)


def solution(mesh):
    placed = (P(None, "row"), P(None, "col")) + (P("row", "col"),) * 6
    return jax.shard_map(
        functools.partial(on_device, mesh.shape["row"], mesh.shape["col"]),
        mesh=mesh,
        in_specs=placed,
        out_specs=(P(None, "row"), P("row", "col"), P("row", "col"), P("row", "col")),
        check_vma=False,
    )
```
